512 devices in a mesh: batch: 32 (over z, core), mp: 16 (over y, x).
Axes of the slice: x: 4, y: 4, z: 16, core: 2. Of those that a mesh axis runs over, the one named last changes fastest.
Arguments:
- queries: bfloat16 [512, 16384], P('batch', 'mp'), may hold values from -384 to 384, as said below
- prompt_cache: bfloat16 [32, 16, 4096, 256], P('batch', 'mp'), may hold values from -48 to 48, as said below
- pool: bfloat16 [1024, 16, 64, 256], P('batch', 'mp'), may hold values from -48 to 48, as said below
- block_table: int32 [512, 4], replicated, may hold values from 0 to 1023, as said below
- parents: int32 [512], replicated, may hold values from 0 to 511, as said below
- lengths: int32 [32], P('batch'), may hold values from 2048 to 8192, as said below
Outputs:
- attended: float32 [512, 16384], P('batch', 'mp')
The draws below stay inside these ranges and needn't reach their ends.
Inputs may be any that keep to these rules, and one draw needn't show every extreme that they name: `queries`: custom float draw of activations; entries stay within the range. `prompt_cache`: keys are of order one and values about eight times larger. `pool`: keys are of order one and values larger, as in prompt_cache. `block_table`: block b is held by batch index b // 32. A row's 4 entries are distinct. The rows of one request name at most 2 distinct blocks held by any one batch index, and exactly 2 held by some index. parents[i] // 16 == i // 16: a row continues a beam of its own request. `lengths`: some request has 8192 valid prompt tokens.
All inputs are finite; a program needn't handle non-finite values.
Results may differ from the reference program's by a relative error of at most 0.007.
Values may be sent and summed in bfloat16 or wider, within the bound.
A program may use at most 64 MiB of HBM per device.

```python
import jax
import jax.numpy as jnp
from jax import lax

HD = 128
GROUP = 16
KVH = 8
NH = 128
BT = 128
PT = 8192
BEAMS = 16
SUF = 4
POOL_DEV = 32
REQ = 32
ROWS = 512


VALUE_SCALE = 8.0


def draw_queries(key, part):
    key = jax.random.fold_in(key, 11)
    first = jax.random.fold_in(key, 0)
    values = jnp.clip(jax.random.normal(first, (ROWS, NH * HD), jnp.float32), -6.0, 6.0)
    return values.astype(jnp.bfloat16)


def draw_prompt_cache(key, part):
    key = jax.random.fold_in(key, 12)
    shape = (REQ, 2 * KVH, PT // 2, 2 * HD)
    entries = jnp.clip(jax.random.normal(key, shape, jnp.float32), -6.0, 6.0)
    column = jnp.arange(2 * HD)
    return (entries * jnp.where(column < HD, 1.0, VALUE_SCALE)).astype(jnp.bfloat16)


def draw_pool(key, part):
    key = jax.random.fold_in(key, 13)
    shape = (REQ * POOL_DEV, 2 * KVH, BT // 2, 2 * HD)
    entries = jnp.clip(jax.random.normal(key, shape, jnp.float32), -6.0, 6.0)
    column = jnp.arange(2 * HD)
    return (entries * jnp.where(column < HD, 1.0, VALUE_SCALE)).astype(jnp.bfloat16)


def draw_block_table(key, part):
    key = jax.random.fold_in(key, 14)
    first, second, third = jax.random.split(key, 3)
    owner_perm = jax.random.permutation(first, REQ)
    slot_perm = jax.vmap(lambda k: jax.random.permutation(k, POOL_DEV))(jax.random.split(second, REQ))
    beam_perm = jax.vmap(lambda k: jax.random.permutation(k, BEAMS))(jax.random.split(third, REQ))
    request = jnp.arange(REQ, dtype=jnp.int32)[:, None]
    columns = []
    for level in range(SUF):
        width = BEAMS // 2 ** (level + 1)
        branch = beam_perm // width
        distinct = 2 ** (level + 1) - 2 + branch
        pair = distinct // 2
        owner = owner_perm[(pair + request) % REQ]
        slot = slot_perm[owner, 2 * pair + distinct % 2]
        columns.append(owner * POOL_DEV + slot)
    table = jnp.stack(columns, axis=-1)
    return table.reshape(ROWS, SUF).astype(jnp.int32)


def draw_parents(key, part):
    key = jax.random.fold_in(key, 15)
    base = jnp.arange(REQ, dtype=jnp.int32)[:, None] * BEAMS
    offset = jax.random.randint(key, (REQ, BEAMS), 0, BEAMS, jnp.int32)
    return (base + offset).reshape(ROWS).astype(jnp.int32)


def draw_lengths(key, part):
    key = jax.random.fold_in(key, 16)
    first, second = jax.random.split(key)
    counts = jax.random.randint(first, (REQ,), PT // 4, PT + 1, jnp.int32)
    longest = jax.random.randint(second, (), 0, REQ, jnp.int32)
    return jnp.where(jnp.arange(REQ, dtype=jnp.int32) == longest, PT, counts).astype(jnp.int32)


def setup_inputs(seed: int = 0) -> dict:
    splits = jax.random.split(jax.random.key(seed), 7)
    return {
        "queries": draw_queries(jax.random.fold_in(splits[6], 71), 0),
        "prompt_cache": draw_prompt_cache(jax.random.fold_in(splits[6], 71), 0),
        "pool": draw_pool(jax.random.fold_in(splits[6], 71), 0),
        "block_table": draw_block_table(jax.random.fold_in(splits[6], 71), 0),
        "parents": draw_parents(jax.random.fold_in(splits[6], 71), 0),
        "lengths": draw_lengths(jax.random.fold_in(splits[6], 71), 0),
    }


big_negative = -1.0e30


def reference(queries, prompt_cache, pool, block_table, parents, lengths):
    half = BT // 2
    scale = HD ** -0.5
    referenced = block_table[parents]
    token = jnp.arange(PT // 2, dtype=jnp.int32)
    side = jnp.arange(2, dtype=jnp.int32)

    def one_request(items):
        rows_q, prompt_r, refs, length = items
        qf = rows_q.astype(jnp.float32).reshape(BEAMS, KVH, GROUP, HD)
        prompt_g = prompt_r.astype(jnp.float32).reshape(KVH, 2, PT // 2, 2 * HD)
        keys_p = prompt_g[..., :HD].reshape(KVH, PT, HD)
        vals_p = prompt_g[..., HD:].reshape(KVH, PT, HD)
        position = (token[None, :] // half) * BT + side[:, None] * half + token[None, :] % half
        valid = (position < length).reshape(PT)
        blocks = pool[refs].astype(jnp.float32)
        blocks = blocks.reshape(BEAMS, SUF, KVH, 2, half, 2 * HD)
        blocks = blocks.transpose(0, 2, 1, 3, 4, 5).reshape(BEAMS, KVH, SUF * BT, 2 * HD)
        keys_s = blocks[..., :HD]
        vals_s = blocks[..., HD:]
        score_p = jnp.einsum('bghd,gtd->bght', qf, keys_p) * scale
        score_p = jnp.where(valid[None, None, None, :], score_p, big_negative)
        score_s = jnp.einsum('bghd,bgtd->bght', qf, keys_s) * scale
        scores = jnp.concatenate([score_p, score_s], axis=-1)
        top = jnp.max(scores, axis=-1, keepdims=True)
        weights = jnp.exp(scores - top)
        total = jnp.sum(weights, axis=-1)
        rounded = lax.optimization_barrier(weights.astype(jnp.bfloat16)).astype(jnp.float32)
        summed = jnp.einsum('bght,gtd->bghd', rounded[..., :PT], vals_p)
        summed = summed + jnp.einsum('bght,bgtd->bghd', rounded[..., PT:], vals_s)
        return (summed / total[..., None]).reshape(BEAMS, KVH * GROUP * HD)

    result = lax.map(one_request, (queries.reshape(REQ, BEAMS, KVH * GROUP * HD), prompt_cache,
                                   referenced.reshape(REQ, BEAMS, SUF), lengths))
    return result.reshape(ROWS, KVH * GROUP * HD)
```

```python
import functools
import math

import jax
import jax.numpy as jnp
from jax import lax
from jax.experimental import pallas as pl
from jax.experimental.pallas import tpu as pltpu
from jax.sharding import PartitionSpec as P

MESH = pl.DeviceIdType.MESH
F32 = jnp.float32
BF16 = jnp.bfloat16

HD = 128
BEAMS = 16
HEADS = 8
NZ = 16
UP = 8
DOWN = 7
SLOTS = 16
HALF = 64
CHUNK = 512
MSG = 144
BIG = -1.0e30
EXPO = HD**-0.5 * math.log2(math.e)

ASK = {1: 0, 2: 1, 3: 2, 4: 3, 5: 0, 6: 5, 7: 6, 8: 7}
BACK = {1: 0, 2: 1, 3: 0, 4: 3, 5: 0, 6: 5, 7: 0, 8: 7}


def slot_of(sign, distance):
    return distance if sign > 0 else UP + distance


def place_of(slot):
    return (1, slot) if slot <= UP else (-1, slot - UP)


def children(table, slot):
    if slot == 0:
        return [s for s in range(1, SLOTS) if table[place_of(s)[1]] == 0]
    sign, distance = place_of(slot)
    return [s for s in range(1, SLOTS) if place_of(s)[0] == sign and table[place_of(s)[1]] == distance]


def iota(shape, dim):
    return lax.broadcasted_iota(jnp.int32, shape, dim)


def split3(value):
    first = value.astype(BF16).astype(F32)
    rest = value - first
    second = rest.astype(BF16).astype(F32)
    return (first, second, rest - second)


def pack(ref, slot, acc, top, total):
    row = iota((16, HD), 0)
    extra = jnp.zeros((16, HD), F32)
    for i, part in enumerate(split3(top) + split3(total)):
        extra = jnp.where(row == i, part, extra)
    ref[slot, 0:HD] = acc.astype(BF16)
    ref[slot, HD:MSG] = extra.astype(BF16)


def unpack(ref, slot):
    extra = ref[slot, HD:MSG].astype(F32)
    top = extra[0:1] + extra[1:2] + extra[2:3]
    total = extra[3:4] + extra[4:5] + extra[5:6]
    return (ref[slot, 0:HD].astype(F32), top, total)


def combine(a, b):
    top = jnp.maximum(a[1], b[1])
    scale_a = jnp.exp2((a[1] - top) * EXPO)
    scale_b = jnp.exp2((b[1] - top) * EXPO)
    return (a[0] * scale_a + b[0] * scale_b, top, a[2] * scale_a + b[2] * scale_b)


def attend(keys, values, vectors, keep):
    scores = jnp.where(keep, jnp.dot(keys, vectors, preferred_element_type=F32), BIG)
    top = jnp.max(scores, axis=0, keepdims=True)
    weights = jnp.where(keep, jnp.exp2((scores - top) * EXPO), 0.0)
    total = jnp.sum(weights, axis=0, keepdims=True)
    acc = lax.dot_general(
        values, weights.astype(BF16), (((0,), (0,)), ((), ())), preferred_element_type=F32
    )
    return (acc, top, total)


def kernel(
    length_ref, q_hbm, prompt_hbm, pool_hbm, table_hbm, parents_hbm, out_ref,
    q_v, prompt_v, pool_v, table_v, parents_v, sel_v, sel_s, keep_v,
    ask_own, ask_pair, part, part_out, part_in, sum_out, sum_in, run_acc, run_row,
    local_sem, prompt_sem, mate_sem, ask_ss, ask_rs, askx_ss, askx_rs, partx_ss, partx_rs, sum_ss, sum_rs,
):
    batch = lax.axis_index("batch")
    mp = lax.axis_index("mp")
    z = batch // 2
    core = batch % 2
    half = mp % 2
    pair = (batch, mp + 1 - 2 * half)
    mate = (batch + 1 - 2 * core, mp)

    def along(offset):
        return ((batch + 2 * (offset % NZ)) % (2 * NZ), mp)

    own_pool = pool_v.at[pl.ds(core * 32, 32)]
    loads = [
        pltpu.make_async_copy(q_hbm, q_v, local_sem.at[0]),
        pltpu.make_async_copy(table_hbm, table_v, local_sem.at[1]),
        pltpu.make_async_copy(parents_hbm, parents_v, local_sem.at[2]),
        pltpu.make_async_copy(pool_hbm, own_pool, local_sem.at[3]),
    ]
    for copy in loads:
        copy.start()
    n_prompt = prompt_v.shape[0] // 1024
    prompt_loads = []
    for i in range(n_prompt):
        rows = pl.ds(i * 1024, 1024)
        prompt_loads.append(
            pltpu.make_async_copy(prompt_hbm.at[rows], prompt_v.at[rows], prompt_sem.at[i])
        )
        prompt_loads[-1].start()

    offsets = set()
    for s in range(1, SLOTS):
        sign, d = place_of(s)
        for table in (ASK, BACK):
            offsets.add(sign * (d - table[d]))
            offsets.add(-sign * (d - table[d]))
    peers = [pair, mate] + [along(o) for o in sorted(offsets)]
    barrier = pltpu.get_barrier_semaphore()
    for peer in peers:
        pl.semaphore_signal(barrier, inc=1, device_id=peer, device_id_type=MESH)

    loads[0].wait()
    stacked = jnp.concatenate([q_v[:, h * HD : (h + 1) * HD] for h in range(HEADS)], axis=0)
    ask_own[0] = stacked.astype(F32).T.astype(BF16)
    pl.semaphore_wait(barrier, len(peers))

    def remote(src, dst, send, recv, device):
        return pltpu.make_async_remote_copy(
            src_ref=src, dst_ref=dst, send_sem=send, recv_sem=recv, device_id=device, device_id_type=MESH
        )

    def ask(slot):
        sign, d = place_of(slot)
        source = 0 if ASK[d] == 0 else slot_of(sign, ASK[d])
        return remote(
            ask_own.at[source], ask_own.at[slot], ask_ss.at[slot], ask_rs.at[slot], along(sign * (d - ASK[d]))
        )

    def askx(slot):
        return remote(ask_own.at[slot], ask_pair.at[slot], askx_ss.at[slot], askx_rs.at[slot], pair)

    def partx(slot):
        return remote(part_out.at[slot], part_in.at[slot], partx_ss.at[slot], partx_rs.at[slot], pair)

    def back(slot):
        sign, d = place_of(slot)
        return remote(
            sum_out.at[slot], sum_in.at[slot], sum_ss.at[slot], sum_rs.at[slot], along(-sign * (d - BACK[d]))
        )

    to_mate = remote(pool_hbm, own_pool, mate_sem.at[0], mate_sem.at[1], mate)

    def hand_on(slot):
        if slot:
            ask(slot).wait_recv()
        for child in sorted(children(ASK, slot), key=lambda s: -place_of(s)[1]):
            ask(child).start()
        askx(slot).start()

    def choose():
        loads[1].wait()
        loads[2].wait()
        n = parents_v.shape[1]
        entry = table_v[...]
        local = jnp.where(entry // 64 == z, entry % 64, -1).astype(F32).astype(BF16)
        picked = jnp.where(parents_v[...] == iota((n, n), 0), 1.0, 0.0).astype(BF16)
        named = jnp.dot(local, picked, preferred_element_type=F32)
        block = iota((64, n), 0).astype(F32)
        hit = jnp.zeros((64, n), F32)
        for j in range(4):
            hit = jnp.where(named[j : j + 1] == block, 1.0, hit)
        group = jnp.where(iota((n, 128), 0) // BEAMS == iota((n, 128), 1), 1.0, 0.0).astype(BF16)
        count = jnp.dot(hit.astype(BF16), group, preferred_element_type=F32)
        number = iota((32, 128), 0)
        row = iota((8, 128), 0)
        chosen = jnp.zeros((8, 128), jnp.int32)
        for owner in range(2):
            got = count[owner * 32 : owner * 32 + 32] > 0.5
            low = jnp.min(jnp.where(got, number, 32), axis=0, keepdims=True)
            low = jnp.where(low > 31, 0, low) + owner * 32
            high = jnp.max(jnp.where(got, number, 0), axis=0, keepdims=True) + owner * 32
            chosen = jnp.where(row == 2 * owner, low, chosen)
            chosen = jnp.where(row == 2 * owner + 1, high, chosen)
        sel_v[...] = chosen
        to_smem = pltpu.make_async_copy(sel_v, sel_s, local_sem.at[4])
        to_smem.start()
        spread = jnp.where(iota((128, n), 1) // BEAMS == iota((128, n), 0), 1.0, 0.0).astype(BF16)
        wide = jnp.dot(chosen.astype(F32).astype(BF16), spread, preferred_element_type=F32)
        uses = jnp.zeros((8, n), F32)
        for j in range(4):
            uses = jnp.where(named[j : j + 1] == wide, 1.0, uses)
        twin = jnp.concatenate([wide[0:1] - 1.0, wide[0:1], wide[2:3] - 1.0, wide[2:3], wide[4:8]], axis=0)
        wide_row = iota((8, n), 0)
        uses = jnp.where((wide == twin) | (wide_row > 3), 0.0, uses)
        tiled = jnp.concatenate([uses] * NZ, axis=0)
        own = iota((8 * NZ, n), 1) // BEAMS == 2 * (iota((8 * NZ, n), 0) // 8) + core
        tile = jnp.where(iota((n, 256), 0) % BEAMS == iota((n, 256), 1) % BEAMS, 1.0, 0.0).astype(BF16)
        rows = jnp.where(own, tiled, 0.0).astype(BF16)
        keep_v[...] = jnp.dot(rows, tile, preferred_element_type=F32)
        to_smem.wait()

    def vectors(slot):
        return jnp.concatenate([ask_own[slot], ask_pair[slot]], axis=1)

    def suffix(slot):
        sign, d = place_of(slot)
        where = (z - sign * d + NZ) % NZ
        request = 2 * where + core
        blocks = [pool_v[sel_s[k, request]] for k in range(4)]
        keys = jnp.concatenate([b[:, :HD] for b in blocks], axis=0)
        values = jnp.concatenate([b[:, HD:] for b in blocks], axis=0)
        rows = keep_v[pl.ds(pl.multiple_of(where * 8, 8), 8), :]
        keep = jnp.concatenate([jnp.broadcast_to(rows[k : k + 1], (HALF, 256)) for k in range(4)], axis=0)
        return attend(keys, values, vectors(slot), keep > 0.5)

    def give(slot, result):
        acc, top, total = result
        part[slot, 0:HD] = acc[:, :HD]
        part[slot, HD : HD + 1] = top[:, :HD]
        part[slot, HD + 1 : HD + 2] = total[:, :HD]
        pack(part_out, slot, acc[:, HD:], top[:, HD:], total[:, HD:])
        partx(slot).start()

    def work(slot):
        askx(slot).wait_recv()
        give(slot, suffix(slot))

    def own_part(slot):
        return (part[slot, 0:HD], part[slot, HD : HD + 1], part[slot, HD + 1 : HD + 2])

    def merge(slot):
        partx(slot).wait_recv()
        result = combine(own_part(slot), unpack(part_in, slot))
        for child in children(BACK, slot):
            back(child).wait_recv()
            result = combine(result, unpack(sum_in, child))
        pack(sum_out, slot, *result)
        back(slot).start()

    def prompt(first, last):
        query = vectors(0)

        def step(i, carry):
            start = pl.multiple_of(i * CHUNK, CHUNK)
            rows = prompt_v[pl.ds(start, CHUNK), :]
            token = start + iota((CHUNK, 256), 0)
            position = token // HALF * (2 * HALF) + half * HALF + token % HALF
            keep = position < length_ref[0]
            result = attend(rows[:, :HD], rows[:, HD:], query, keep)
            acc, top, total = combine((run_acc[...], run_row[0:1], run_row[1:2]), result)
            run_acc[...] = acc
            run_row[0:1] = top
            run_row[1:2] = total
            return carry

        lax.fori_loop(first, last, step, 0)

    def both(*distances):
        return [slot_of(sign, d) for d in distances for sign in (1, -1) if sign > 0 or d <= DOWN]

    hand_on(0)
    to_mate.start()
    run_acc[...] = jnp.zeros_like(run_acc)
    run_row[0:1] = jnp.full((1, 256), BIG, F32)
    run_row[1:2] = jnp.zeros((1, 256), F32)
    choose()
    for s in both(1):
        hand_on(s)
    askx(0).wait_recv()
    for copy in prompt_loads:
        copy.wait()
    prompt(0, 4)
    for s in both(5, 2):
        hand_on(s)
    loads[3].wait()
    to_mate.wait()
    for s in both(1):
        work(s)
    prompt(4, 6)
    for s in both(6, 3):
        hand_on(s)
    for s in both(5, 2):
        work(s)
    for s in both(7, 4):
        hand_on(s)
    for s in both(6, 3):
        work(s)
    for s in both(5, 2):
        if s in both(2):
            merge(s)
    for s in both(8):
        hand_on(s)
    for s in both(7, 4):
        work(s)
    for s in both(6):
        merge(s)
    for s in both(1):
        merge(s)
    for s in both(8):
        work(s)
    for s in both(4):
        merge(s)
    for s in both(5):
        merge(s)
    prompt(6, 8)
    give(0, combine((run_acc[...], run_row[0:1], run_row[1:2]), suffix(0)))
    for s in both(8, 3, 7):
        merge(s)
    partx(0).wait_recv()
    result = combine(own_part(0), unpack(part_in, 0))
    for s in both(1, 5, 3, 7):
        back(s).wait_recv()
        result = combine(result, unpack(sum_in, s))
    final = (result[0] / result[2]).T
    for h in range(HEADS):
        out_ref[:, h * HD : (h + 1) * HD] = final[h * BEAMS : (h + 1) * BEAMS, :]
    for s in range(SLOTS):
        askx(s).wait_send()
        partx(s).wait_send()
        if s:
            ask(s).wait_send()
            back(s).wait_send()


def on_device(queries, prompt_cache, pool, block_table, parents, lengths):
    rows = block_table.shape[0]
    any_space = pl.BlockSpec(memory_space=pl.ANY)
    dma = pltpu.SemaphoreType.DMA
    return pl.pallas_call(
        kernel,
        out_shape=jax.ShapeDtypeStruct((BEAMS, HEADS * HD), F32),
        in_specs=[pl.BlockSpec(memory_space=pltpu.SMEM)] + [any_space] * 5,
        out_specs=pl.BlockSpec(memory_space=pltpu.VMEM),
        scratch_shapes=[
            pltpu.VMEM((BEAMS, HEADS * HD), BF16),
            pltpu.VMEM((4096, 2 * HD), BF16),
            pltpu.VMEM((64, HALF, 2 * HD), BF16),
            pltpu.VMEM((4, rows), jnp.int32),
            pltpu.VMEM((1, rows), jnp.int32),
            pltpu.VMEM((8, 128), jnp.int32),
            pltpu.SMEM((8, 128), jnp.int32),
            pltpu.VMEM((8 * NZ, 256), F32),
            pltpu.VMEM((SLOTS, HD, HD), BF16),
            pltpu.VMEM((SLOTS, HD, HD), BF16),
            pltpu.VMEM((SLOTS, HD + 8, HD), F32),
            pltpu.VMEM((SLOTS, MSG, HD), BF16),
            pltpu.VMEM((SLOTS, MSG, HD), BF16),
            pltpu.VMEM((SLOTS, MSG, HD), BF16),
            pltpu.VMEM((SLOTS, MSG, HD), BF16),
            pltpu.VMEM((HD, 256), F32),
            pltpu.VMEM((8, 256), F32),
            dma((5,)),
            dma((4,)),
            dma((2,)),
        ]
        + [dma((SLOTS,))] * 8,
        compiler_params=pltpu.CompilerParams(
            collective_id=0, has_side_effects=True, vmem_limit_bytes=48 * 1024 * 1024
        ),
        name="carried_queries",
    )(
        lengths,
        queries,
        prompt_cache[0, 0],
        pool[:, 0],
        block_table.T,
        parents.reshape(1, rows),
    )


def solution(mesh):
    return jax.shard_map(
        on_device,
        mesh=mesh,
        in_specs=(
            P("batch", "mp"),
            P("batch", "mp", None, None),
            P("batch", "mp", None, None),
            P(),
            P(),
            P("batch"),
        ),
        out_specs=P("batch", "mp"),
        check_vma=False,
    )
```

```python
import functools
import math

import jax
import jax.numpy as jnp
from jax import lax
from jax.experimental import pallas as pl
from jax.experimental.pallas import tpu as pltpu
from jax.sharding import PartitionSpec as P

MESH = pl.DeviceIdType.MESH
F32 = jnp.float32
BF16 = jnp.bfloat16

HD = 128
BEAMS = 16
HEADS = 8
NZ = 16
UP = 8
DOWN = 7
SLOTS = 16
HALF = 64
CHUNK = 512
MSG = 144
BIG = -1.0e30
EXPO = HD**-0.5 * math.log2(math.e)
OWN, OTHER = slice(0, HD), slice(HD, 2 * HD)

ASK = {1: 0, 2: 1, 3: 2, 4: 3, 5: 0, 6: 5, 7: 6, 8: 7}
BACK = {1: 0, 2: 1, 3: 0, 4: 3, 5: 0, 6: 5, 7: 0, 8: 7}
ASK_WIDE = ()
BACK_WIDE = (2, 4, 6, 8)
ORDER = (
    ("h", 0), ("c", 0), ("p", 0), ("p", 1), ("p", 2), ("p", 3), ("p", 4), ("w", 0), ("p", 5), ("p", 6),
    ("h", 1), ("h", 9), ("p", 7), ("p", 8), ("p", 9), ("p", 10), ("p", 11), ("a", 0), ("h", 5), ("h", 13),
    ("p", 12), ("h", 2), ("h", 10), ("w", 1), ("a", 1), ("w", 9), ("a", 9), ("p", 13), ("p", 14), ("p", 15),
    ("o", 0), ("w", 5), ("h", 6), ("h", 14), ("a", 5), ("w", 13), ("h", 3), ("h", 11), ("a", 13), ("w", 2),
    ("a", 2), ("w", 10), ("o", 2), ("a", 10), ("o", 10), ("h", 7), ("h", 15), ("w", 6), ("a", 6), ("h", 4),
    ("h", 12), ("w", 14), ("o", 6), ("a", 14), ("w", 3), ("o", 14), ("a", 3), ("w", 11), ("a", 11), ("o", 1),
    ("w", 7), ("a", 7), ("o", 9), ("w", 15), ("a", 15), ("h", 8), ("o", 15), ("w", 4), ("a", 4), ("o", 4),
    ("w", 12), ("a", 12), ("o", 5), ("o", 12), ("o", 13), ("m", 1), ("m", 9), ("w", 8), ("a", 8), ("o", 8),
    ("m", 15), ("m", 5), ("o", 3), ("m", 13), ("o", 11), ("o", 7), ("m", 3), ("m", 11), ("m", 7), ("m", 0),
)


LAST = (1, 9, 3, 11, 5, 13, 7, 15)


def slot_of(sign, distance):
    return distance if sign > 0 else UP + distance


def place_of(slot):
    return (1, slot) if slot <= UP else (-1, slot - UP)


def children(table, slot):
    if slot == 0:
        return [s for s in range(1, SLOTS) if table[place_of(s)[1]] == 0]
    sign, distance = place_of(slot)
    return [s for s in range(1, SLOTS) if place_of(s)[0] == sign and table[place_of(s)[1]] == distance]


def wide_ask(slot):
    return slot > 0 and place_of(slot)[1] in ASK_WIDE


def wide_back(slot):
    return slot > 0 and place_of(slot)[1] in BACK_WIDE


def iota(shape, dim):
    return lax.broadcasted_iota(jnp.int32, shape, dim)


def split3(value):
    first = value.astype(BF16).astype(F32)
    rest = value - first
    second = rest.astype(BF16).astype(F32)
    return (first, second, rest - second)


def pack(ref, result):
    acc, top, total = result
    row = iota((16, HD), 0)
    extra = jnp.zeros((16, HD), F32)
    for i, value in enumerate(split3(top) + split3(total)):
        extra = jnp.where(row == i, value, extra)
    ref[0:HD] = acc.astype(BF16)
    ref[HD:MSG] = extra.astype(BF16)


def unpack(ref):
    extra = ref[HD:MSG].astype(F32)
    top = extra[0:1] + extra[1:2] + extra[2:3]
    total = extra[3:4] + extra[4:5] + extra[5:6]
    return (ref[0:HD].astype(F32), top, total)


def combine(a, b):
    top = jnp.maximum(a[1], b[1])
    scale_a = jnp.exp2((a[1] - top) * EXPO)
    scale_b = jnp.exp2((b[1] - top) * EXPO)
    return (a[0] * scale_a + b[0] * scale_b, top, a[2] * scale_a + b[2] * scale_b)


def attend(keys, values, vectors, mask):
    scores = mask(jnp.dot(keys, vectors, preferred_element_type=F32))
    top = jnp.max(scores, axis=0, keepdims=True)
    weights = jnp.exp2((scores - top) * EXPO)
    total = jnp.sum(weights, axis=0, keepdims=True)
    acc = lax.dot_general(
        values, weights.astype(BF16), (((0,), (0,)), ((), ())), preferred_element_type=F32
    )
    return (acc, top, total)


def kernel(
    length_ref, q_hbm, prompt_hbm, pool_hbm, table_hbm, parents_hbm, out_ref,
    q_v, prompt_v, pool_v, table_v, parents_v, sel_v, sel_s, keep_v,
    ask_own, ask_pair, part, part_out, part_in, sum_out, sum_in, run,
    local_sem, prompt_sem, mate_sem, ask_ss, ask_rs, askw_ss, askw_rs, askx_ss, askx_rs, partx_ss, partx_rs, sum_ss, sum_rs,
):
    batch = lax.axis_index("batch")
    mp = lax.axis_index("mp")
    z = batch // 2
    core = batch % 2
    half = mp % 2
    pair = (batch, mp + 1 - 2 * half)
    mate = (batch + 1 - 2 * core, mp)

    def along(offset):
        return ((batch + 2 * (offset % NZ)) % (2 * NZ), mp)

    own_pool = pool_v.at[pl.ds(core * 32, 32)]
    loads = [
        pltpu.make_async_copy(q_hbm, q_v, local_sem.at[0]),
        pltpu.make_async_copy(table_hbm, table_v, local_sem.at[1]),
        pltpu.make_async_copy(parents_hbm, parents_v, local_sem.at[2]),
        pltpu.make_async_copy(pool_hbm, own_pool, local_sem.at[3]),
    ]
    for copy in loads:
        copy.start()
    n_prompt = prompt_v.shape[0] // 1024
    prompt_loads = []
    for i in range(n_prompt):
        rows = pl.ds(i * 1024, 1024)
        prompt_loads.append(
            pltpu.make_async_copy(prompt_hbm.at[rows], prompt_v.at[rows], prompt_sem.at[i])
        )
        prompt_loads[-1].start()

    offsets = set()
    for s in range(1, SLOTS):
        sign, d = place_of(s)
        for table in (ASK,):
            offsets.add(sign * (d - table[d]))
            offsets.add(-sign * (d - table[d]))
    peers = [pair, mate] + [along(o) for o in sorted(offsets)]
    barrier = pltpu.get_barrier_semaphore()
    for peer in peers:
        pl.semaphore_signal(barrier, inc=1, device_id=peer, device_id_type=MESH)

    loads[0].wait()
    stacked = jnp.concatenate([q_v[:, h * HD : (h + 1) * HD] for h in range(HEADS)], axis=0)
    ask_own[0] = stacked.astype(F32).T.astype(BF16)

    def remote(src, dst, send, recv, device):
        return pltpu.make_async_remote_copy(
            src_ref=src, dst_ref=dst, send_sem=send, recv_sem=recv, device_id=device, device_id_type=MESH
        )

    def came(table, slot):
        sign, d = place_of(slot)
        source = table[d]
        return (slot_of(sign, source) if source else 0, sign * (source - d))

    def ask(slot):
        source, offset = came(ASK, slot)
        return remote(ask_own.at[source], ask_own.at[slot], ask_ss.at[slot], ask_rs.at[slot], along(-offset))

    def askw(slot):
        source, offset = came(ASK, slot)
        return remote(ask_pair.at[source], ask_pair.at[slot], askw_ss.at[slot], askw_rs.at[slot], along(-offset))

    def askx(slot):
        return remote(ask_own.at[slot], ask_pair.at[slot], askx_ss.at[slot], askx_rs.at[slot], pair)

    def partx(slot):
        return remote(part_out.at[slot], part_in.at[slot], partx_ss.at[slot], partx_rs.at[slot], pair)

    def back(slot):
        _, offset = came(BACK, slot)
        sides = pl.ds(0, 2 if wide_back(slot) else 1)
        return remote(
            sum_out.at[slot, sides], sum_in.at[slot, sides], sum_ss.at[slot], sum_rs.at[slot], along(offset)
        )

    to_mate = remote(pool_hbm, own_pool, mate_sem.at[0], mate_sem.at[1], mate)

    def far_first(slots):
        return sorted(slots, key=lambda s: -place_of(s)[1])

    def hand_own(slot):
        if slot:
            ask(slot).wait_recv()
        for child in far_first(children(ASK, slot)):
            ask(child).start()
        if not wide_ask(slot):
            askx(slot).start()

    def hand_pair(slot):
        (askw if wide_ask(slot) else askx)(slot).wait_recv()
        for child in far_first(children(ASK, slot)):
            if wide_ask(child):
                askw(child).start()

    def choose():
        loads[1].wait()
        loads[2].wait()
        n = parents_v.shape[1]
        entry = table_v[...]
        local = jnp.where(entry // 64 == z, entry % 64, -1).astype(F32).astype(BF16)
        picked = jnp.where(parents_v[...] == iota((n, n), 0), 1.0, 0.0).astype(BF16)
        named = jnp.dot(local, picked, preferred_element_type=F32)
        block = iota((64, n), 0).astype(F32)
        hit = jnp.zeros((64, n), F32)
        for j in range(4):
            hit = jnp.where(named[j : j + 1] == block, 1.0, hit)
        group = jnp.where(iota((n, 128), 0) // BEAMS == iota((n, 128), 1), 1.0, 0.0).astype(BF16)
        count = jnp.dot(hit.astype(BF16), group, preferred_element_type=F32)
        number = iota((32, 128), 0)
        row = iota((8, 128), 0)
        chosen = jnp.zeros((8, 128), jnp.int32)
        for owner in range(2):
            got = count[owner * 32 : owner * 32 + 32] > 0.5
            low = jnp.min(jnp.where(got, number, 32), axis=0, keepdims=True)
            low = jnp.where(low > 31, 0, low) + owner * 32
            high = jnp.max(jnp.where(got, number, 0), axis=0, keepdims=True) + owner * 32
            chosen = jnp.where(row == 2 * owner, low, chosen)
            chosen = jnp.where(row == 2 * owner + 1, high, chosen)
        sel_v[...] = chosen
        to_smem = pltpu.make_async_copy(sel_v, sel_s, local_sem.at[4])
        to_smem.start()
        spread = jnp.where(iota((128, n), 1) // BEAMS == iota((128, n), 0), 1.0, 0.0).astype(BF16)
        wide = jnp.dot(chosen.astype(F32).astype(BF16), spread, preferred_element_type=F32)
        uses = jnp.zeros((8, n), F32)
        for j in range(4):
            uses = jnp.where(named[j : j + 1] == wide, 1.0, uses)
        twin = jnp.concatenate([wide[0:1] - 1.0, wide[0:1], wide[2:3] - 1.0, wide[2:3], wide[4:8]], axis=0)
        wide_row = iota((8, n), 0)
        uses = jnp.where((wide == twin) | (wide_row > 3), 0.0, uses)
        tiled = jnp.concatenate([uses] * NZ, axis=0)
        own = iota((8 * NZ, n), 1) // BEAMS == 2 * (iota((8 * NZ, n), 0) // 8) + core
        tile = jnp.where(iota((n, 256), 0) % BEAMS == iota((n, 256), 1) % BEAMS, 1.0, 0.0).astype(BF16)
        rows = jnp.where(own, tiled, 0.0).astype(BF16)
        keep_v[...] = jnp.where(jnp.dot(rows, tile, preferred_element_type=F32) > 0.5, 0.0, BIG)
        to_smem.wait()

    def vectors(slot):
        return jnp.concatenate([ask_own[slot], ask_pair[slot]], axis=1)

    def suffix(slot):
        sign, d = place_of(slot)
        where = (z - sign * d + NZ) % NZ
        request = 2 * where + core
        blocks = [pool_v[sel_s[k, request]] for k in range(4)]
        keys = jnp.concatenate([b[:, :HD] for b in blocks], axis=0)
        values = jnp.concatenate([b[:, HD:] for b in blocks], axis=0)
        rows = keep_v[pl.ds(pl.multiple_of(where * 8, 8), 8), :]

        def mask(scores):
            return jnp.concatenate(
                [scores[k * HALF : (k + 1) * HALF] + rows[k : k + 1] for k in range(4)], axis=0
            )

        return attend(keys, values, vectors(slot), mask)

    def keep_sums(slot, result):
        part[slot, 0:HD] = result[0]
        part[slot, HD : HD + 1] = result[1]
        part[slot, HD + 1 : HD + 2] = result[2]

    def kept_sums(slot, lanes):
        return (part[slot, 0:HD, lanes], part[slot, HD : HD + 1, lanes], part[slot, HD + 1 : HD + 2, lanes])

    def work(slot):
        result = suffix(slot)
        keep_sums(slot, result)

    def send_on(slot):
        own, other = kept_sums(slot, OWN), kept_sums(slot, OTHER)
        if slot == 0:
            own = combine(own, (run[0:HD, OWN], run[HD : HD + 1, OWN], run[HD + 1 : HD + 2, OWN]))
            other = combine(other, (run[0:HD, OTHER], run[HD : HD + 1, OTHER], run[HD + 1 : HD + 2, OTHER]))
        grown = slot == 0
        for child in children(BACK, slot):
            if wide_back(child):
                back(child).wait_recv()
                own = combine(own, unpack(sum_in.at[child, 0]))
                other = combine(other, unpack(sum_in.at[child, 1]))
                grown = True
        if wide_back(slot):
            pack(sum_out.at[slot, 0], own)
            pack(sum_out.at[slot, 1], other)
            back(slot).start()
        else:
            pack(part_out.at[slot], other)
            partx(slot).start()
            if grown:
                part[slot, 0:HD, OWN] = own[0]
                part[slot, HD : HD + 1, OWN] = own[1]
                part[slot, HD + 1 : HD + 2, OWN] = own[2]

    def merge(slot):
        partx(slot).wait_recv()
        result = combine(kept_sums(slot, OWN), unpack(part_in.at[slot]))
        for child in LAST if slot == 0 else children(BACK, slot):
            if not wide_back(child):
                back(child).wait_recv()
                result = combine(result, unpack(sum_in.at[child, 0]))
        if slot:
            pack(sum_out.at[slot, 0], result)
            back(slot).start()
        return result

    def prompt(i, side):
        lanes = slice(side * HD, (side + 1) * HD)
        start = pl.multiple_of(i * CHUNK, CHUNK)
        rows = prompt_v[pl.ds(start, CHUNK), :]
        inside = iota((HALF, HD), 0)

        def mask(scores):
            parts = []
            for k in range(CHUNK // HALF):
                room = length_ref[0] - 2 * start - (2 * k + half) * HALF
                parts.append(jnp.where(inside < room, scores[k * HALF : (k + 1) * HALF], BIG))
            return jnp.concatenate(parts, axis=0)

        result = attend(rows[:, :HD], rows[:, HD:], (ask_pair if side else ask_own)[0], mask)
        result = combine((run[0:HD, lanes], run[HD : HD + 1, lanes], run[HD + 1 : HD + 2, lanes]), result)
        run[0:HD, lanes] = result[0]
        run[HD : HD + 1, lanes] = result[1]
        run[HD + 1 : HD + 2, lanes] = result[2]

    run[...] = jnp.zeros_like(run)
    run[HD : HD + 1] = jnp.full((1, 256), BIG, F32)
    pl.semaphore_wait(barrier, len(peers))

    chunks = prompt_v.shape[0] // CHUNK
    loaded = set()
    for kind, s in ORDER:
        if kind == "h":
            hand_own(s)
            if s == 0:
                to_mate.start()
        elif kind == "w":
            hand_pair(s)
        elif kind == "c":
            choose()
        elif kind == "a":
            if "pool" not in loaded:
                loads[3].wait()
                to_mate.wait()
                loaded.add("pool")
            work(s)
        elif kind == "o":
            send_on(s)
        elif kind == "p":
            piece = s % chunks * CHUNK // 1024
            if piece not in loaded:
                prompt_loads[piece].wait()
                loaded.add(piece)
            prompt(s % chunks, s // chunks)
        elif kind == "m" and s:
            merge(s)
    result = merge(0)
    final = (result[0] / result[2]).T
    for h in range(HEADS):
        out_ref[:, h * HD : (h + 1) * HD] = final[h * BEAMS : (h + 1) * BEAMS, :]
    for s in range(SLOTS):
        if not wide_ask(s):
            askx(s).wait_send()
        if not wide_back(s):
            partx(s).wait_send()
        if s:
            ask(s).wait_send()
            back(s).wait_send()
            if wide_ask(s):
                askw(s).wait_send()


def on_device(queries, prompt_cache, pool, block_table, parents, lengths):
    rows = block_table.shape[0]
    any_space = pl.BlockSpec(memory_space=pl.ANY)
    dma = pltpu.SemaphoreType.DMA
    return pl.pallas_call(
        kernel,
        out_shape=jax.ShapeDtypeStruct((BEAMS, HEADS * HD), F32),
        in_specs=[pl.BlockSpec(memory_space=pltpu.SMEM)] + [any_space] * 5,
        out_specs=pl.BlockSpec(memory_space=pltpu.VMEM),
        scratch_shapes=[
            pltpu.VMEM((BEAMS, HEADS * HD), BF16),
            pltpu.VMEM((4096, 2 * HD), BF16),
            pltpu.VMEM((64, HALF, 2 * HD), BF16),
            pltpu.VMEM((4, rows), jnp.int32),
            pltpu.VMEM((1, rows), jnp.int32),
            pltpu.VMEM((8, 128), jnp.int32),
            pltpu.SMEM((8, 128), jnp.int32),
            pltpu.VMEM((8 * NZ, 256), F32),
            pltpu.VMEM((SLOTS, HD, HD), BF16),
            pltpu.VMEM((SLOTS, HD, HD), BF16),
            pltpu.VMEM((SLOTS, HD + 8, 2 * HD), F32),
            pltpu.VMEM((SLOTS, MSG, HD), BF16),
            pltpu.VMEM((SLOTS, MSG, HD), BF16),
            pltpu.VMEM((SLOTS, 2, MSG, HD), BF16),
            pltpu.VMEM((SLOTS, 2, MSG, HD), BF16),
            pltpu.VMEM((HD + 8, 2 * HD), F32),
            dma((5,)),
            dma((4,)),
            dma((2,)),
        ]
        + [dma((SLOTS,))] * 10,
        compiler_params=pltpu.CompilerParams(
            collective_id=0, has_side_effects=True, vmem_limit_bytes=60 * 1024 * 1024
        ),
        name="carried_queries",
    )(
        lengths,
        queries,
        prompt_cache[0, 0],
        pool[:, 0],
        block_table.T,
        parents.reshape(1, rows),
    )


def solution(mesh):
    return jax.shard_map(
        on_device,
        mesh=mesh,
        in_specs=(
            P("batch", "mp"),
            P("batch", "mp", None, None),
            P("batch", "mp", None, None),
            P(),
            P(),
            P("batch"),
        ),
        out_specs=P("batch", "mp"),
        check_vma=False,
    )
```

```python
import functools
import math

import jax
import jax.numpy as jnp
from jax import lax
from jax.experimental import pallas as pl
from jax.experimental.pallas import tpu as pltpu
from jax.sharding import PartitionSpec as P

MESH = pl.DeviceIdType.MESH
F32 = jnp.float32
BF16 = jnp.bfloat16

HD = 128
BEAMS = 16
HEADS = 8
NZ = 16
UP = 8
DOWN = 7
SLOTS = 16
HALF = 64
CHUNK = 512
MSG = 144
EARLY = NZ // 2
BIG = -1.0e30
EXPO = HD**-0.5 * math.log2(math.e)
OWN, OTHER = slice(0, HD), slice(HD, 2 * HD)

ASK = {1: 0, 2: 4, 3: 1, 4: 5, 5: 0, 6: 4, 7: 5, 8: 5}
BACK = {1: 2, 2: 0, 3: 2, 4: 2, 5: 6, 6: 0, 7: 6, 8: 6}
ASK_WIDE = (3, 4)
BACK_WIDE = (4, 7)
ORDER = (
    ("h", 0), ("c", 0), ("p", 0), ("p", 1), ("p", 2), ("p", 3), ("p", 4), ("w", 0), ("p", 5), ("p", 6),
    ("h", 1), ("h", 9), ("p", 7), ("p", 8), ("p", 9), ("p", 10), ("p", 11), ("a", 0), ("h", 5), ("h", 13),
    ("p", 12), ("w", 1), ("a", 1), ("o", 1), ("h", 3), ("h", 11), ("w", 9), ("a", 9), ("o", 9), ("p", 13),
    ("p", 14), ("p", 15), ("w", 5), ("h", 4), ("o", 0), ("a", 5), ("w", 13), ("o", 5), ("a", 13), ("h", 15),
    ("h", 12), ("m", 1), ("o", 13), ("m", 9), ("w", 11), ("a", 11), ("o", 11), ("h", 7), ("w", 4), ("a", 4),
    ("o", 4), ("h", 8), ("m", 5), ("w", 3), ("h", 2), ("a", 3), ("w", 15), ("o", 3), ("a", 15), ("w", 12),
    ("m", 13), ("o", 15), ("a", 12), ("h", 14), ("m", 11), ("o", 12), ("w", 7), ("a", 7), ("o", 7), ("w", 8),
    ("h", 6), ("a", 8), ("w", 2), ("h", 10), ("o", 8), ("a", 2), ("m", 3), ("o", 2), ("w", 14), ("a", 14),
    ("o", 14), ("w", 6), ("a", 6), ("w", 10), ("o", 6), ("a", 10), ("m", 8), ("m", 2), ("m", 14), ("o", 10),
    ("m", 6), ("m", 10),
)


LAST = (2, 10, 6, 14)


def slot_of(sign, distance):
    return distance if sign > 0 else UP + distance


def place_of(slot):
    return (1, slot) if slot <= UP else (-1, slot - UP)


def children(table, slot):
    if slot == 0:
        return [s for s in range(1, SLOTS) if table[place_of(s)[1]] == 0]
    sign, distance = place_of(slot)
    return [s for s in range(1, SLOTS) if place_of(s)[0] == sign and table[place_of(s)[1]] == distance]


def wide_ask(slot):
    return slot > 0 and place_of(slot)[1] in ASK_WIDE


def wide_back(slot):
    return slot > 0 and place_of(slot)[1] in BACK_WIDE


def iota(shape, dim):
    return lax.broadcasted_iota(jnp.int32, shape, dim)


def split3(value):
    first = value.astype(BF16).astype(F32)
    rest = value - first
    second = rest.astype(BF16).astype(F32)
    return (first, second, rest - second)


def pack(ref, result):
    acc, top, total = result
    row = iota((16, HD), 0)
    extra = jnp.zeros((16, HD), F32)
    for i, value in enumerate(split3(top) + split3(total)):
        extra = jnp.where(row == i, value, extra)
    ref[0:HD] = acc.astype(BF16)
    ref[HD:MSG] = extra.astype(BF16)


def unpack(ref):
    extra = ref[HD:MSG].astype(F32)
    top = extra[0:1] + extra[1:2] + extra[2:3]
    total = extra[3:4] + extra[4:5] + extra[5:6]
    return (ref[0:HD].astype(F32), top, total)


def combine(a, b):
    top = jnp.maximum(a[1], b[1])
    scale_a = jnp.exp2((a[1] - top) * EXPO)
    scale_b = jnp.exp2((b[1] - top) * EXPO)
    return (a[0] * scale_a + b[0] * scale_b, top, a[2] * scale_a + b[2] * scale_b)


def attend(keys, values, vectors, mask):
    scores = mask(jnp.dot(keys, vectors, preferred_element_type=F32))
    top = jnp.max(scores, axis=0, keepdims=True)
    weights = jnp.exp2((scores - top) * EXPO)
    total = jnp.sum(weights, axis=0, keepdims=True)
    acc = lax.dot_general(
        values, weights.astype(BF16), (((0,), (0,)), ((), ())), preferred_element_type=F32
    )
    return (acc, top, total)


def kernel(
    length_ref, q_hbm, prompt_hbm, pool_hbm, table_hbm, parents_hbm, out_ref,
    q_v, prompt_v, pool_v, table_v, parents_v, sel_v, sel_s, keep_v,
    ask_own, ask_pair, part, part_out, part_in, sum_out, sum_in, run,
    local_sem, prompt_sem, mate_sem, ask_ss, ask_rs, askw_ss, askw_rs, askx_ss, askx_rs, partx_ss, partx_rs, sum_ss, sum_rs,
):
    batch = lax.axis_index("batch")
    mp = lax.axis_index("mp")
    z = batch // 2
    core = batch % 2
    half = mp % 2
    pair = (batch, mp + 1 - 2 * half)
    mate = (batch + 1 - 2 * core, mp)

    def along(offset):
        return ((batch + 2 * (offset % NZ)) % (2 * NZ), mp)

    own_pool = pool_v.at[pl.ds(core * 32, 32)]
    loads = [
        pltpu.make_async_copy(q_hbm, q_v, local_sem.at[0]),
        pltpu.make_async_copy(table_hbm, table_v, local_sem.at[1]),
        pltpu.make_async_copy(parents_hbm, parents_v, local_sem.at[2]),
        pltpu.make_async_copy(pool_hbm, own_pool, local_sem.at[3]),
    ]
    for copy in loads:
        copy.start()
    n_prompt = prompt_v.shape[0] // 1024
    prompt_loads = []
    for i in range(n_prompt):
        rows = pl.ds(i * 1024, 1024)
        prompt_loads.append(
            pltpu.make_async_copy(prompt_hbm.at[rows], prompt_v.at[rows], prompt_sem.at[i])
        )
        prompt_loads[-1].start()

    offsets = set()
    for s in range(1, SLOTS):
        sign, d = place_of(s)
        for table in (ASK,):
            offsets.add(sign * (d - table[d]))
            offsets.add(-sign * (d - table[d]))
    peers = [pair, mate] + [along(o) for o in sorted(offsets)]
    barrier = pltpu.get_barrier_semaphore()
    for peer in peers:
        pl.semaphore_signal(barrier, inc=1, device_id=peer, device_id_type=MESH)

    loads[0].wait()
    stacked = jnp.concatenate([q_v[:, h * HD : (h + 1) * HD] for h in range(HEADS)], axis=0)
    ask_own[0] = stacked.astype(F32).T.astype(BF16)

    def remote(src, dst, send, recv, device):
        return pltpu.make_async_remote_copy(
            src_ref=src, dst_ref=dst, send_sem=send, recv_sem=recv, device_id=device, device_id_type=MESH
        )

    def came(table, slot):
        sign, d = place_of(slot)
        source = table[d]
        return (slot_of(sign, source) if source else 0, sign * (source - d))

    def ask(slot):
        source, offset = came(ASK, slot)
        return remote(ask_own.at[source], ask_own.at[slot], ask_ss.at[slot], ask_rs.at[slot], along(-offset))

    def askw(slot):
        source, offset = came(ASK, slot)
        return remote(ask_pair.at[source], ask_pair.at[slot], askw_ss.at[slot], askw_rs.at[slot], along(-offset))

    def askx(slot):
        return remote(ask_own.at[slot], ask_pair.at[slot], askx_ss.at[slot], askx_rs.at[slot], pair)

    def partx(slot):
        return remote(part_out.at[slot], part_in.at[slot], partx_ss.at[slot], partx_rs.at[slot], pair)

    def back(slot):
        _, offset = came(BACK, slot)
        sides = pl.ds(0, 2 if wide_back(slot) else 1)
        return remote(
            sum_out.at[slot, sides], sum_in.at[slot, sides], sum_ss.at[slot], sum_rs.at[slot], along(offset)
        )

    to_mate = remote(pool_hbm, own_pool, mate_sem.at[0], mate_sem.at[1], mate)

    def far_first(slots):
        return sorted(slots, key=lambda s: -place_of(s)[1])

    def hand_own(slot):
        if slot:
            ask(slot).wait_recv()
        for child in far_first(children(ASK, slot)):
            ask(child).start()
        if not wide_ask(slot):
            askx(slot).start()

    def hand_pair(slot):
        (askw if wide_ask(slot) else askx)(slot).wait_recv()
        for child in far_first(children(ASK, slot)):
            if wide_ask(child):
                askw(child).start()

    def choose():
        loads[1].wait()
        loads[2].wait()
        n = parents_v.shape[1]
        entry = table_v[...]
        local = jnp.where(entry // 64 == z, entry % 64, -1).astype(F32).astype(BF16)
        picked = jnp.where(parents_v[...] == iota((n, n), 0), 1.0, 0.0).astype(BF16)
        named = jnp.dot(local, picked, preferred_element_type=F32)
        block = iota((64, n), 0).astype(F32)
        hit = jnp.zeros((64, n), F32)
        for j in range(4):
            hit = jnp.where(named[j : j + 1] == block, 1.0, hit)
        group = jnp.where(iota((n, 128), 0) // BEAMS == iota((n, 128), 1), 1.0, 0.0).astype(BF16)
        count = jnp.dot(hit.astype(BF16), group, preferred_element_type=F32)
        number = iota((32, 128), 0)
        row = iota((8, 128), 0)
        chosen = jnp.zeros((8, 128), jnp.int32)
        for owner in range(2):
            got = count[owner * 32 : owner * 32 + 32] > 0.5
            low = jnp.min(jnp.where(got, number, 32), axis=0, keepdims=True)
            low = jnp.where(low > 31, 0, low) + owner * 32
            high = jnp.max(jnp.where(got, number, 0), axis=0, keepdims=True) + owner * 32
            chosen = jnp.where(row == 2 * owner, low, chosen)
            chosen = jnp.where(row == 2 * owner + 1, high, chosen)
        sel_v[...] = chosen
        to_smem = pltpu.make_async_copy(sel_v, sel_s, local_sem.at[4])
        to_smem.start()
        spread = jnp.where(iota((128, n), 1) // BEAMS == iota((128, n), 0), 1.0, 0.0).astype(BF16)
        wide = jnp.dot(chosen.astype(F32).astype(BF16), spread, preferred_element_type=F32)
        uses = jnp.zeros((8, n), F32)
        for j in range(4):
            uses = jnp.where(named[j : j + 1] == wide, 1.0, uses)
        twin = jnp.concatenate([wide[0:1] - 1.0, wide[0:1], wide[2:3] - 1.0, wide[2:3], wide[4:8]], axis=0)
        wide_row = iota((8, n), 0)
        uses = jnp.where((wide == twin) | (wide_row > 3), 0.0, uses)
        tiled = jnp.concatenate([uses] * NZ, axis=0)
        own = iota((8 * NZ, n), 1) // BEAMS == 2 * (iota((8 * NZ, n), 0) // 8) + core
        tile = jnp.where(iota((n, 256), 0) % BEAMS == iota((n, 256), 1) % BEAMS, 1.0, 0.0).astype(BF16)
        rows = jnp.where(own, tiled, 0.0).astype(BF16)
        keep_v[...] = jnp.where(jnp.dot(rows, tile, preferred_element_type=F32) > 0.5, 0.0, BIG)
        to_smem.wait()

    def vectors(slot):
        return jnp.concatenate([ask_own[slot], ask_pair[slot]], axis=1)

    def suffix(slot):
        sign, d = place_of(slot)
        where = (z - sign * d + NZ) % NZ
        request = 2 * where + core
        blocks = [pool_v[sel_s[k, request]] for k in range(4)]
        keys = jnp.concatenate([b[:, :HD] for b in blocks], axis=0)
        values = jnp.concatenate([b[:, HD:] for b in blocks], axis=0)
        rows = keep_v[pl.ds(pl.multiple_of(where * 8, 8), 8), :]

        def mask(scores):
            return jnp.concatenate(
                [scores[k * HALF : (k + 1) * HALF] + rows[k : k + 1] for k in range(4)], axis=0
            )

        return attend(keys, values, vectors(slot), mask)

    def keep_sums(slot, result):
        part[slot, 0:HD] = result[0]
        part[slot, HD : HD + 1] = result[1]
        part[slot, HD + 1 : HD + 2] = result[2]

    def kept_sums(slot, lanes):
        return (part[slot, 0:HD, lanes], part[slot, HD : HD + 1, lanes], part[slot, HD + 1 : HD + 2, lanes])

    def work(slot):
        result = suffix(slot)
        keep_sums(slot, result)

    def send_on(slot):
        own, other = kept_sums(slot, OWN), kept_sums(slot, OTHER)
        if slot == 0:
            own = combine(own, (run[0:HD, OWN], run[HD : HD + 1, OWN], run[HD + 1 : HD + 2, OWN]))
            other = combine(other, (run[0:HD, OTHER], run[HD : HD + 1, OTHER], run[HD + 1 : HD + 2, OTHER]))
        grown = slot == 0
        for child in children(BACK, slot):
            if wide_back(child):
                back(child).wait_recv()
                own = combine(own, unpack(sum_in.at[child, 0]))
                other = combine(other, unpack(sum_in.at[child, 1]))
                grown = True
        if wide_back(slot):
            pack(sum_out.at[slot, 0], own)
            pack(sum_out.at[slot, 1], other)
            back(slot).start()
        else:
            pack(part_out.at[slot], other)
            partx(slot).start()
            if grown:
                part[slot, 0:HD, OWN] = own[0]
                part[slot, HD : HD + 1, OWN] = own[1]
                part[slot, HD + 1 : HD + 2, OWN] = own[2]

    def merge(slot):
        partx(slot).wait_recv()
        result = combine(kept_sums(slot, OWN), unpack(part_in.at[slot]))
        for child in LAST if slot == 0 else children(BACK, slot):
            if not wide_back(child):
                back(child).wait_recv()
                result = combine(result, unpack(sum_in.at[child, 0]))
        if slot:
            pack(sum_out.at[slot, 0], result)
            back(slot).start()
        return result

    def prompt(i, side):
        lanes = slice(side * HD, (side + 1) * HD)
        start = pl.multiple_of(i * CHUNK, CHUNK)
        rows = prompt_v[pl.ds(start, CHUNK), :]
        inside = iota((HALF, HD), 0)

        def mask(scores):
            parts = []
            for k in range(CHUNK // HALF):
                room = length_ref[0] - 2 * start - (2 * k + half) * HALF
                parts.append(jnp.where(inside < room, scores[k * HALF : (k + 1) * HALF], BIG))
            return jnp.concatenate(parts, axis=0)

        result = attend(rows[:, :HD], rows[:, HD:], (ask_pair if side else ask_own)[0], mask)
        result = combine((run[0:HD, lanes], run[HD : HD + 1, lanes], run[HD + 1 : HD + 2, lanes]), result)
        run[0:HD, lanes] = result[0]
        run[HD : HD + 1, lanes] = result[1]
        run[HD + 1 : HD + 2, lanes] = result[2]

    run[...] = jnp.zeros_like(run)
    run[HD : HD + 1] = jnp.full((1, 256), BIG, F32)
    chunks = prompt_v.shape[0] // CHUNK
    early = z < EARLY

    @pl.when(early)
    def _():
        choose()
        for i, copy in enumerate(prompt_loads):
            copy.wait()
            for k in range(i * 1024 // CHUNK, (i + 1) * 1024 // CHUNK):
                prompt(k, 0)

    pl.semaphore_wait(barrier, len(peers))
    loaded = set()
    for kind, s in ORDER:
        if kind == "h":
            hand_own(s)
            if s == 0:
                to_mate.start()
        elif kind == "w":
            hand_pair(s)
        elif kind == "c":
            pl.when(~early)(choose)
        elif kind == "a":
            if "pool" not in loaded:
                loads[3].wait()
                to_mate.wait()
                loaded.add("pool")
            work(s)
        elif kind == "o":
            send_on(s)
        elif kind == "p":
            piece = s % chunks * CHUNK // 1024
            if s < chunks:

                @pl.when(~early)
                def _():
                    if piece not in loaded:
                        prompt_loads[piece].wait()
                    prompt(s, 0)

                loaded.add(piece)
            else:
                prompt(s - chunks, 1)
        elif kind == "m" and s:
            merge(s)
    result = merge(0)
    final = (result[0] / result[2]).T
    for h in range(HEADS):
        out_ref[:, h * HD : (h + 1) * HD] = final[h * BEAMS : (h + 1) * BEAMS, :]
    for s in range(SLOTS):
        if not wide_ask(s):
            askx(s).wait_send()
        if not wide_back(s):
            partx(s).wait_send()
        if s:
            ask(s).wait_send()
            back(s).wait_send()
            if wide_ask(s):
                askw(s).wait_send()


def on_device(queries, prompt_cache, pool, block_table, parents, lengths):
    rows = block_table.shape[0]
    any_space = pl.BlockSpec(memory_space=pl.ANY)
    dma = pltpu.SemaphoreType.DMA
    return pl.pallas_call(
        kernel,
        out_shape=jax.ShapeDtypeStruct((BEAMS, HEADS * HD), F32),
        in_specs=[pl.BlockSpec(memory_space=pltpu.SMEM)] + [any_space] * 5,
        out_specs=pl.BlockSpec(memory_space=pltpu.VMEM),
        scratch_shapes=[
            pltpu.VMEM((BEAMS, HEADS * HD), BF16),
            pltpu.VMEM((4096, 2 * HD), BF16),
            pltpu.VMEM((64, HALF, 2 * HD), BF16),
            pltpu.VMEM((4, rows), jnp.int32),
            pltpu.VMEM((1, rows), jnp.int32),
            pltpu.VMEM((8, 128), jnp.int32),
            pltpu.SMEM((8, 128), jnp.int32),
            pltpu.VMEM((8 * NZ, 256), F32),
            pltpu.VMEM((SLOTS, HD, HD), BF16),
            pltpu.VMEM((SLOTS, HD, HD), BF16),
            pltpu.VMEM((SLOTS, HD + 8, 2 * HD), F32),
            pltpu.VMEM((SLOTS, MSG, HD), BF16),
            pltpu.VMEM((SLOTS, MSG, HD), BF16),
            pltpu.VMEM((SLOTS, 2, MSG, HD), BF16),
            pltpu.VMEM((SLOTS, 2, MSG, HD), BF16),
            pltpu.VMEM((HD + 8, 2 * HD), F32),
            dma((5,)),
            dma((4,)),
            dma((2,)),
        ]
        + [dma((SLOTS,))] * 10,
        compiler_params=pltpu.CompilerParams(
            collective_id=0, has_side_effects=True, vmem_limit_bytes=60 * 1024 * 1024
        ),
        name="carried_queries",
    )(
        lengths,
        queries,
        prompt_cache[0, 0],
        pool[:, 0],
        block_table.T,
        parents.reshape(1, rows),
    )


def solution(mesh):
    return jax.shard_map(
        on_device,
        mesh=mesh,
        in_specs=(
            P("batch", "mp"),
            P("batch", "mp", None, None),
            P("batch", "mp", None, None),
            P(),
            P(),
            P("batch"),
        ),
        out_specs=P("batch", "mp"),
        check_vma=False,
    )
```

```python
import functools
import math

import jax
import jax.numpy as jnp
from jax import lax
from jax.experimental import pallas as pl
from jax.experimental.pallas import tpu as pltpu
from jax.sharding import PartitionSpec as P

MESH = pl.DeviceIdType.MESH
F32 = jnp.float32
BF16 = jnp.bfloat16

HD = 128
BEAMS = 16
HEADS = 8
NZ = 16
UP = 8
DOWN = 7
SLOTS = 16
HALF = 64
CHUNK = 512
MSG = 144
EARLY = NZ // 2
BIG = -1.0e30
EXPO = HD**-0.5 * math.log2(math.e)
OWN, OTHER = slice(0, HD), slice(HD, 2 * HD)

ASK = {1: 0, 2: 4, 3: 1, 4: 5, 5: 0, 6: 4, 7: 5, 8: 5}
BACK = {1: 2, 2: 0, 3: 2, 4: 2, 5: 6, 6: 0, 7: 6, 8: 6}
ASK_WIDE = (3, 4)
BACK_WIDE = (4, 7)
ORDER = (
    ("h", 0), ("c", 0), ("p", 0), ("p", 1), ("p", 2), ("p", 3), ("p", 4), ("w", 0), ("p", 5), ("p", 6),
    ("h", 1), ("h", 9), ("p", 7), ("p", 8), ("p", 9), ("p", 10), ("p", 11), ("a", 0), ("h", 5), ("h", 13),
    ("p", 12), ("w", 1), ("a", 1), ("o", 1), ("h", 3), ("h", 11), ("w", 9), ("a", 9), ("o", 9), ("p", 13),
    ("p", 14), ("p", 15), ("w", 5), ("h", 4), ("o", 0), ("a", 5), ("w", 13), ("o", 5), ("a", 13), ("h", 15),
    ("h", 12), ("m", 1), ("o", 13), ("m", 9), ("w", 11), ("a", 11), ("o", 11), ("h", 7), ("w", 4), ("a", 4),
    ("o", 4), ("h", 8), ("m", 5), ("w", 3), ("h", 2), ("a", 3), ("w", 15), ("o", 3), ("a", 15), ("w", 12),
    ("m", 13), ("o", 15), ("a", 12), ("h", 14), ("m", 11), ("o", 12), ("w", 7), ("a", 7), ("o", 7), ("w", 8),
    ("h", 6), ("a", 8), ("w", 2), ("h", 10), ("o", 8), ("a", 2), ("m", 3), ("o", 2), ("w", 14), ("a", 14),
    ("o", 14), ("w", 6), ("a", 6), ("w", 10), ("o", 6), ("a", 10), ("m", 8), ("m", 2), ("m", 14), ("o", 10),
    ("m", 6), ("m", 10),
)


LAST = (2, 10, 6, 14)


def slot_of(sign, distance):
    return distance if sign > 0 else UP + distance


def place_of(slot):
    return (1, slot) if slot <= UP else (-1, slot - UP)


def children(table, slot):
    if slot == 0:
        return [s for s in range(1, SLOTS) if table[place_of(s)[1]] == 0]
    sign, distance = place_of(slot)
    return [s for s in range(1, SLOTS) if place_of(s)[0] == sign and table[place_of(s)[1]] == distance]


def wide_ask(slot):
    return slot > 0 and place_of(slot)[1] in ASK_WIDE


def wide_back(slot):
    return slot > 0 and place_of(slot)[1] in BACK_WIDE


def iota(shape, dim):
    return lax.broadcasted_iota(jnp.int32, shape, dim)


def split3(value):
    first = value.astype(BF16).astype(F32)
    rest = value - first
    second = rest.astype(BF16).astype(F32)
    return (first, second, rest - second)


def pack(ref, result):
    acc, top, total = result
    row = iota((16, HD), 0)
    extra = jnp.zeros((16, HD), F32)
    for i, value in enumerate(split3(top) + split3(total)):
        extra = jnp.where(row == i, value, extra)
    ref[0:HD] = acc.astype(BF16)
    ref[HD:MSG] = extra.astype(BF16)


def unpack(ref):
    extra = ref[HD:MSG].astype(F32)
    top = extra[0:1] + extra[1:2] + extra[2:3]
    total = extra[3:4] + extra[4:5] + extra[5:6]
    return (ref[0:HD].astype(F32), top, total)


def combine(a, b):
    top = jnp.maximum(a[1], b[1])
    scale_a = jnp.exp2((a[1] - top) * EXPO)
    scale_b = jnp.exp2((b[1] - top) * EXPO)
    return (a[0] * scale_a + b[0] * scale_b, top, a[2] * scale_a + b[2] * scale_b)


def attend(keys, values, vectors, mask):
    scores = mask(jnp.dot(keys, vectors, preferred_element_type=F32))
    top = jnp.max(scores, axis=0, keepdims=True)
    weights = jnp.exp2((scores - top) * EXPO)
    total = jnp.sum(weights, axis=0, keepdims=True)
    acc = lax.dot_general(
        values, weights.astype(BF16), (((0,), (0,)), ((), ())), preferred_element_type=F32
    )
    return (acc, top, total)


def kernel(
    length_ref, q_hbm, prompt_hbm, pool_hbm, table_hbm, parents_hbm, out_ref,
    q_v, prompt_v, pool_v, table_v, parents_v, sel_v, sel_s, keep_v,
    ask_own, ask_pair, part, part_out, part_in, sum_out, sum_in, run,
    local_sem, prompt_sem, mate_sem, ask_ss, ask_rs, askw_ss, askw_rs, askx_ss, askx_rs, partx_ss, partx_rs, sum_ss, sum_rs,
):
    batch = lax.axis_index("batch")
    mp = lax.axis_index("mp")
    z = batch // 2
    core = batch % 2
    half = mp % 2
    pair = (batch, mp + 1 - 2 * half)
    mate = (batch + 1 - 2 * core, mp)

    def along(offset):
        return ((batch + 2 * (offset % NZ)) % (2 * NZ), mp)

    own_pool = pool_v.at[pl.ds(core * 32, 32)]
    loads = [
        pltpu.make_async_copy(q_hbm, q_v, local_sem.at[0]),
        pltpu.make_async_copy(table_hbm, table_v, local_sem.at[1]),
        pltpu.make_async_copy(parents_hbm, parents_v, local_sem.at[2]),
        pltpu.make_async_copy(pool_hbm, own_pool, local_sem.at[3]),
    ]
    for copy in loads:
        copy.start()
    n_prompt = prompt_v.shape[0] // 1024
    prompt_loads = []
    for i in range(n_prompt):
        rows = pl.ds(i * 1024, 1024)
        prompt_loads.append(
            pltpu.make_async_copy(prompt_hbm.at[rows], prompt_v.at[rows], prompt_sem.at[i])
        )
        prompt_loads[-1].start()

    offsets = set()
    for s in range(1, SLOTS):
        sign, d = place_of(s)
        for table in (ASK,):
            offsets.add(sign * (d - table[d]))
            offsets.add(-sign * (d - table[d]))
    peers = [pair, mate] + [along(o) for o in sorted(offsets)]
    barrier = pltpu.get_barrier_semaphore()
    for peer in peers:
        pl.semaphore_signal(barrier, inc=1, device_id=peer, device_id_type=MESH)

    loads[0].wait()
    stacked = jnp.concatenate([q_v[:, h * HD : (h + 1) * HD] for h in range(HEADS)], axis=0)
    ask_own[0] = stacked.astype(F32).T.astype(BF16)

    def remote(src, dst, send, recv, device):
        return pltpu.make_async_remote_copy(
            src_ref=src, dst_ref=dst, send_sem=send, recv_sem=recv, device_id=device, device_id_type=MESH
        )

    def came(table, slot):
        sign, d = place_of(slot)
        source = table[d]
        return (slot_of(sign, source) if source else 0, sign * (source - d))

    def ask(slot):
        source, offset = came(ASK, slot)
        return remote(ask_own.at[source], ask_own.at[slot], ask_ss.at[slot], ask_rs.at[slot], along(-offset))

    def askw(slot):
        source, offset = came(ASK, slot)
        return remote(ask_pair.at[source], ask_pair.at[slot], askw_ss.at[slot], askw_rs.at[slot], along(-offset))

    def askx(slot):
        return remote(ask_own.at[slot], ask_pair.at[slot], askx_ss.at[slot], askx_rs.at[slot], pair)

    def partx(slot):
        return remote(part_out.at[slot], part_in.at[slot], partx_ss.at[slot], partx_rs.at[slot], pair)

    def back(slot):
        _, offset = came(BACK, slot)
        sides = pl.ds(0, 2 if wide_back(slot) else 1)
        return remote(
            sum_out.at[slot, sides], sum_in.at[slot, sides], sum_ss.at[slot], sum_rs.at[slot], along(offset)
        )

    to_mate = remote(pool_hbm, own_pool, mate_sem.at[0], mate_sem.at[1], mate)

    def far_first(slots):
        return sorted(slots, key=lambda s: -place_of(s)[1])

    def hand_own(slot):
        if slot:
            ask(slot).wait_recv()
        for child in far_first(children(ASK, slot)):
            ask(child).start()
        if not wide_ask(slot):
            askx(slot).start()

    def hand_pair(slot):
        (askw if wide_ask(slot) else askx)(slot).wait_recv()
        for child in far_first(children(ASK, slot)):
            if wide_ask(child):
                askw(child).start()

    def choose():
        loads[1].wait()
        loads[2].wait()
        n = parents_v.shape[1]
        entry = table_v[...]
        local = jnp.where(entry // 64 == z, entry % 64, -1).astype(F32).astype(BF16)
        picked = jnp.where(parents_v[...] == iota((n, n), 0), 1.0, 0.0).astype(BF16)
        named = jnp.dot(local, picked, preferred_element_type=F32)
        block = iota((64, n), 0).astype(F32)
        hit = jnp.zeros((64, n), F32)
        for j in range(4):
            hit = jnp.where(named[j : j + 1] == block, 1.0, hit)
        group = jnp.where(iota((n, 128), 0) // BEAMS == iota((n, 128), 1), 1.0, 0.0).astype(BF16)
        count = jnp.dot(hit.astype(BF16), group, preferred_element_type=F32)
        number = iota((32, 128), 0)
        row = iota((8, 128), 0)
        chosen = jnp.zeros((8, 128), jnp.int32)
        for owner in range(2):
            got = count[owner * 32 : owner * 32 + 32] > 0.5
            low = jnp.min(jnp.where(got, number, 32), axis=0, keepdims=True)
            low = jnp.where(low > 31, 0, low) + owner * 32
            high = jnp.max(jnp.where(got, number, 0), axis=0, keepdims=True) + owner * 32
            chosen = jnp.where(row == 2 * owner, low, chosen)
            chosen = jnp.where(row == 2 * owner + 1, high, chosen)
        sel_v[...] = chosen
        to_smem = pltpu.make_async_copy(sel_v, sel_s, local_sem.at[4])
        to_smem.start()
        spread = jnp.where(iota((128, n), 1) // BEAMS == iota((128, n), 0), 1.0, 0.0).astype(BF16)
        wide = jnp.dot(chosen.astype(F32).astype(BF16), spread, preferred_element_type=F32)
        uses = jnp.zeros((8, n), F32)
        for j in range(4):
            uses = jnp.where(named[j : j + 1] == wide, 1.0, uses)
        twin = jnp.concatenate([wide[0:1] - 1.0, wide[0:1], wide[2:3] - 1.0, wide[2:3], wide[4:8]], axis=0)
        wide_row = iota((8, n), 0)
        uses = jnp.where((wide == twin) | (wide_row > 3), 0.0, uses)
        tiled = jnp.concatenate([uses] * NZ, axis=0)
        own = iota((8 * NZ, n), 1) // BEAMS == 2 * (iota((8 * NZ, n), 0) // 8) + core
        tile = jnp.where(iota((n, 256), 0) % BEAMS == iota((n, 256), 1) % BEAMS, 1.0, 0.0).astype(BF16)
        rows = jnp.where(own, tiled, 0.0).astype(BF16)
        keep_v[...] = jnp.where(jnp.dot(rows, tile, preferred_element_type=F32) > 0.5, 0.0, BIG)
        to_smem.wait()

    def vectors(slot):
        return jnp.concatenate([ask_own[slot], ask_pair[slot]], axis=1)

    def suffix(slot):
        sign, d = place_of(slot)
        where = (z - sign * d + NZ) % NZ
        request = 2 * where + core
        blocks = [pool_v[sel_s[k, request]] for k in range(4)]
        keys = jnp.concatenate([b[:, :HD] for b in blocks], axis=0)
        values = jnp.concatenate([b[:, HD:] for b in blocks], axis=0)
        rows = keep_v[pl.ds(pl.multiple_of(where * 8, 8), 8), :]

        def mask(scores):
            return jnp.concatenate(
                [scores[k * HALF : (k + 1) * HALF] + rows[k : k + 1] for k in range(4)], axis=0
            )

        return attend(keys, values, vectors(slot), mask)

    def keep_sums(slot, result):
        part[slot, 0:HD] = result[0]
        part[slot, HD : HD + 1] = result[1]
        part[slot, HD + 1 : HD + 2] = result[2]

    def kept_sums(slot, lanes):
        return (part[slot, 0:HD, lanes], part[slot, HD : HD + 1, lanes], part[slot, HD + 1 : HD + 2, lanes])

    def work(slot):
        result = suffix(slot)
        keep_sums(slot, result)

    def send_on(slot):
        own, other = kept_sums(slot, OWN), kept_sums(slot, OTHER)
        if slot == 0:
            own = combine(own, (run[0:HD, OWN], run[HD : HD + 1, OWN], run[HD + 1 : HD + 2, OWN]))
            other = combine(other, (run[0:HD, OTHER], run[HD : HD + 1, OTHER], run[HD + 1 : HD + 2, OTHER]))
        grown = slot == 0
        for child in children(BACK, slot):
            if wide_back(child):
                back(child).wait_recv()
                own = combine(own, unpack(sum_in.at[child, 0]))
                other = combine(other, unpack(sum_in.at[child, 1]))
                grown = True
        if wide_back(slot):
            pack(sum_out.at[slot, 0], own)
            pack(sum_out.at[slot, 1], other)
            back(slot).start()
        else:
            pack(part_out.at[slot], other)
            partx(slot).start()
            if grown:
                part[slot, 0:HD, OWN] = own[0]
                part[slot, HD : HD + 1, OWN] = own[1]
                part[slot, HD + 1 : HD + 2, OWN] = own[2]

    def merge(slot):
        partx(slot).wait_recv()
        result = combine(kept_sums(slot, OWN), unpack(part_in.at[slot]))
        for child in LAST if slot == 0 else children(BACK, slot):
            if not wide_back(child):
                back(child).wait_recv()
                result = combine(result, unpack(sum_in.at[child, 0]))
        if slot:
            pack(sum_out.at[slot, 0], result)
            back(slot).start()
        return result

    def prompt(i, side):
        lanes = slice(side * HD, (side + 1) * HD)
        start = pl.multiple_of(i * CHUNK, CHUNK)
        rows = prompt_v[pl.ds(start, CHUNK), :]
        inside = iota((HALF, HD), 0)

        def mask(scores):
            parts = []
            for k in range(CHUNK // HALF):
                room = length_ref[0] - 2 * start - (2 * k + half) * HALF
                parts.append(jnp.where(inside < room, scores[k * HALF : (k + 1) * HALF], BIG))
            return jnp.concatenate(parts, axis=0)

        result = attend(rows[:, :HD], rows[:, HD:], (ask_pair if side else ask_own)[0], mask)
        result = combine((run[0:HD, lanes], run[HD : HD + 1, lanes], run[HD + 1 : HD + 2, lanes]), result)
        run[0:HD, lanes] = result[0]
        run[HD : HD + 1, lanes] = result[1]
        run[HD + 1 : HD + 2, lanes] = result[2]

    run[...] = jnp.zeros_like(run)
    run[HD : HD + 1] = jnp.full((1, 256), BIG, F32)
    chunks = prompt_v.shape[0] // CHUNK
    early = z < EARLY

    @pl.when(early)
    def _():
        choose()
        for i, copy in enumerate(prompt_loads):
            copy.wait()
            for k in range(i * 1024 // CHUNK, (i + 1) * 1024 // CHUNK):
                prompt(k, 0)

    pl.semaphore_wait(barrier, len(peers))
    loaded = set()
    for kind, s in ORDER:
        if kind == "h":
            hand_own(s)
            if s == 0:
                to_mate.start()
        elif kind == "w":
            hand_pair(s)
        elif kind == "c":
            pl.when(~early)(choose)
        elif kind == "a":
            if "pool" not in loaded:
                loads[3].wait()
                to_mate.wait()
                loaded.add("pool")
            work(s)
        elif kind == "o":
            send_on(s)
        elif kind == "p":
            piece = s % chunks * CHUNK // 1024
            if s < chunks:

                @pl.when(~early)
                def _():
                    if piece not in loaded:
                        prompt_loads[piece].wait()
                    prompt(s, 0)

                loaded.add(piece)
            else:
                prompt(s - chunks, 1)
        elif kind == "m" and s:
            merge(s)
    result = merge(0)
    final = (result[0] / result[2]).T
    for h in range(HEADS):
        out_ref[:, h * HD : (h + 1) * HD] = final[h * BEAMS : (h + 1) * BEAMS, :]
    for s in range(SLOTS):
        if not wide_ask(s):
            askx(s).wait_send()
        if not wide_back(s):
            partx(s).wait_send()
        if s:
            ask(s).wait_send()
            back(s).wait_send()
            if wide_ask(s):
                askw(s).wait_send()


def on_device(queries, prompt_cache, pool, block_table, parents, lengths):
    rows = block_table.shape[0]
    any_space = pl.BlockSpec(memory_space=pl.ANY)
    dma = pltpu.SemaphoreType.DMA
    return pl.pallas_call(
        kernel,
        out_shape=pltpu.VMEM((BEAMS, HEADS * HD), F32),
        in_specs=[pl.BlockSpec(memory_space=pltpu.SMEM)] + [any_space] * 5,
        out_specs=pl.BlockSpec(memory_space=pltpu.VMEM),
        scratch_shapes=[
            pltpu.VMEM((BEAMS, HEADS * HD), BF16),
            pltpu.VMEM((4096, 2 * HD), BF16),
            pltpu.VMEM((64, HALF, 2 * HD), BF16),
            pltpu.VMEM((4, rows), jnp.int32),
            pltpu.VMEM((1, rows), jnp.int32),
            pltpu.VMEM((8, 128), jnp.int32),
            pltpu.SMEM((8, 128), jnp.int32),
            pltpu.VMEM((8 * NZ, 256), F32),
            pltpu.VMEM((SLOTS, HD, HD), BF16),
            pltpu.VMEM((SLOTS, HD, HD), BF16),
            pltpu.VMEM((SLOTS, HD + 8, 2 * HD), F32),
            pltpu.VMEM((SLOTS, MSG, HD), BF16),
            pltpu.VMEM((SLOTS, MSG, HD), BF16),
            pltpu.VMEM((SLOTS, 2, MSG, HD), BF16),
            pltpu.VMEM((SLOTS, 2, MSG, HD), BF16),
            pltpu.VMEM((HD + 8, 2 * HD), F32),
            dma((5,)),
            dma((4,)),
            dma((2,)),
        ]
        + [dma((SLOTS,))] * 10,
        compiler_params=pltpu.CompilerParams(
            collective_id=0, has_side_effects=True, vmem_limit_bytes=54 * 1024 * 1024
        ),
        name="carried_queries",
    )(
        lengths,
        queries,
        prompt_cache[0, 0],
        pool[:, 0],
        block_table.T,
        parents.reshape(1, rows),
    )


def solution(mesh):
    return jax.shard_map(
        on_device,
        mesh=mesh,
        in_specs=(
            P("batch", "mp"),
            P("batch", "mp", None, None),
            P("batch", "mp", None, None),
            P(),
            P(),
            P("batch"),
        ),
        out_specs=P("batch", "mp"),
        check_vma=False,
    )
```

```python
import functools
import math

import jax
import jax.numpy as jnp
from jax import lax
from jax.experimental import pallas as pl
from jax.experimental.pallas import tpu as pltpu
from jax.sharding import PartitionSpec as P

MESH = pl.DeviceIdType.MESH
F32 = jnp.float32
BF16 = jnp.bfloat16

HD = 128
BEAMS = 16
HEADS = 8
NZ = 16
UP = 8
DOWN = 7
SLOTS = 16
HALF = 64
CHUNK = 512
MSG = 144
EARLY = NZ // 2
BIG = -1.0e30
EXPO = HD**-0.5 * math.log2(math.e)
OWN, OTHER = slice(0, HD), slice(HD, 2 * HD)

ASK = {1: 2, 2: 0, 3: 2, 4: 0, 5: 4, 6: 5, 7: 4, 8: 7}
BACK = {1: 0, 2: 3, 3: 0, 4: 5, 5: 6, 6: 0, 7: 6, 8: 6}
ASK_WIDE = (3, 6, 8)
BACK_WIDE = (2, 4, 5, 7)
ORDER = (
    ("h", 0), ("c", 0), ("w", 0), ("p", 15), ("p", 10), ("p", 8), ("p", 9), ("h", 2), ("p", 1), ("h", 10),
    ("h", 4), ("h", 12), ("p", 3), ("p", 12), ("p", 0), ("p", 5), ("h", 9), ("w", 2), ("p", 4), ("w", 10),
    ("a", 2), ("h", 11), ("o", 2), ("h", 5), ("w", 4), ("w", 12), ("h", 3), ("a", 10), ("a", 4), ("h", 7),
    ("a", 12), ("h", 13), ("o", 12), ("o", 4), ("w", 9), ("a", 9), ("h", 15), ("o", 9), ("w", 5), ("h", 1),
    ("w", 3), ("o", 10), ("a", 0), ("a", 5), ("w", 7), ("a", 3), ("w", 13), ("w", 11), ("a", 13), ("a", 7),
    ("p", 14), ("h", 8), ("w", 15), ("a", 15), ("o", 15), ("o", 13), ("o", 3), ("w", 1), ("w", 8), ("a", 8),
    ("o", 8), ("o", 7), ("o", 5), ("a", 11), ("p", 13), ("o", 11), ("a", 1), ("h", 14), ("m", 9), ("w", 14),
    ("a", 14), ("o", 1), ("p", 7), ("m", 8), ("h", 6), ("o", 14), ("m", 3), ("w", 6), ("a", 6), ("o", 6),
    ("m", 11), ("m", 1), ("p", 2), ("p", 11), ("m", 14), ("p", 6), ("o", 0), ("m", 6),
)


LAST = (1, 9, 3, 11, 6, 14)


def slot_of(sign, distance):
    return distance if sign > 0 else UP + distance


def place_of(slot):
    return (1, slot) if slot <= UP else (-1, slot - UP)


def children(table, slot):
    if slot == 0:
        return [s for s in range(1, SLOTS) if table[place_of(s)[1]] == 0]
    sign, distance = place_of(slot)
    return [s for s in range(1, SLOTS) if place_of(s)[0] == sign and table[place_of(s)[1]] == distance]


def wide_ask(slot):
    return slot > 0 and place_of(slot)[1] in ASK_WIDE


def wide_back(slot):
    return slot > 0 and place_of(slot)[1] in BACK_WIDE


def iota(shape, dim):
    return lax.broadcasted_iota(jnp.int32, shape, dim)


def split3(value):
    first = value.astype(BF16).astype(F32)
    rest = value - first
    second = rest.astype(BF16).astype(F32)
    return (first, second, rest - second)


def pack(ref, result):
    acc, top, total = result
    row = iota((16, HD), 0)
    extra = jnp.zeros((16, HD), F32)
    for i, value in enumerate(split3(top) + split3(total)):
        extra = jnp.where(row == i, value, extra)
    ref[0:HD] = acc.astype(BF16)
    ref[HD:MSG] = extra.astype(BF16)


def unpack(ref):
    extra = ref[HD:MSG].astype(F32)
    top = extra[0:1] + extra[1:2] + extra[2:3]
    total = extra[3:4] + extra[4:5] + extra[5:6]
    return (ref[0:HD].astype(F32), top, total)


def combine(a, b):
    top = jnp.maximum(a[1], b[1])
    scale_a = jnp.exp2((a[1] - top) * EXPO)
    scale_b = jnp.exp2((b[1] - top) * EXPO)
    return (a[0] * scale_a + b[0] * scale_b, top, a[2] * scale_a + b[2] * scale_b)


def attend(keys, values, vectors, mask):
    scores = mask(jnp.dot(keys, vectors, preferred_element_type=F32))
    top = jnp.max(scores, axis=0, keepdims=True)
    weights = jnp.exp2((scores - top) * EXPO)
    total = jnp.sum(weights, axis=0, keepdims=True)
    acc = lax.dot_general(
        values, weights.astype(BF16), (((0,), (0,)), ((), ())), preferred_element_type=F32
    )
    return (acc, top, total)


def kernel(
    length_ref, q_hbm, prompt_hbm, pool_hbm, table_hbm, parents_hbm, out_ref,
    q_v, prompt_v, pool_v, table_v, parents_v, sel_v, sel_s, keep_v,
    ask_own, ask_pair, part, part_out, part_in, sum_out, sum_in, run,
    local_sem, prompt_sem, mate_sem, ask_ss, ask_rs, askw_ss, askw_rs, askx_ss, askx_rs, partx_ss, partx_rs, sum_ss, sum_rs,
):
    batch = lax.axis_index("batch")
    mp = lax.axis_index("mp")
    z = batch // 2
    core = batch % 2
    half = mp % 2
    pair = (batch, mp + 1 - 2 * half)
    mate = (batch + 1 - 2 * core, mp)

    def along(offset):
        return ((batch + 2 * (offset % NZ)) % (2 * NZ), mp)

    own_pool = pool_v.at[pl.ds(core * 32, 32)]
    loads = [
        pltpu.make_async_copy(q_hbm, q_v, local_sem.at[0]),
        pltpu.make_async_copy(table_hbm, table_v, local_sem.at[1]),
        pltpu.make_async_copy(parents_hbm, parents_v, local_sem.at[2]),
        pltpu.make_async_copy(pool_hbm, own_pool, local_sem.at[3]),
    ]
    for copy in loads:
        copy.start()
    n_prompt = prompt_v.shape[0] // 1024
    prompt_loads = []
    for i in range(n_prompt):
        rows = pl.ds(i * 1024, 1024)
        prompt_loads.append(
            pltpu.make_async_copy(prompt_hbm.at[rows], prompt_v.at[rows], prompt_sem.at[i])
        )
        prompt_loads[-1].start()

    offsets = set()
    for s in range(1, SLOTS):
        sign, d = place_of(s)
        for table in (ASK,):
            offsets.add(sign * (d - table[d]))
            offsets.add(-sign * (d - table[d]))
    peers = [pair, mate] + [along(o) for o in sorted(offsets)]
    barrier = pltpu.get_barrier_semaphore()
    for peer in peers:
        pl.semaphore_signal(barrier, inc=1, device_id=peer, device_id_type=MESH)

    loads[0].wait()
    stacked = jnp.concatenate([q_v[:, h * HD : (h + 1) * HD] for h in range(HEADS)], axis=0)
    ask_own[0] = stacked.astype(F32).T.astype(BF16)

    def remote(src, dst, send, recv, device):
        return pltpu.make_async_remote_copy(
            src_ref=src, dst_ref=dst, send_sem=send, recv_sem=recv, device_id=device, device_id_type=MESH
        )

    def came(table, slot):
        sign, d = place_of(slot)
        source = table[d]
        return (slot_of(sign, source) if source else 0, sign * (source - d))

    def ask(slot):
        source, offset = came(ASK, slot)
        return remote(ask_own.at[source], ask_own.at[slot], ask_ss.at[slot], ask_rs.at[slot], along(-offset))

    def askw(slot):
        source, offset = came(ASK, slot)
        return remote(ask_pair.at[source], ask_pair.at[slot], askw_ss.at[slot], askw_rs.at[slot], along(-offset))

    def askx(slot):
        return remote(ask_own.at[slot], ask_pair.at[slot], askx_ss.at[slot], askx_rs.at[slot], pair)

    def partx(slot):
        return remote(part_out.at[slot], part_in.at[slot], partx_ss.at[slot], partx_rs.at[slot], pair)

    def back(slot):
        _, offset = came(BACK, slot)
        sides = pl.ds(0, 2 if wide_back(slot) else 1)
        return remote(
            sum_out.at[slot, sides], sum_in.at[slot, sides], sum_ss.at[slot], sum_rs.at[slot], along(offset)
        )

    to_mate = remote(pool_hbm, own_pool, mate_sem.at[0], mate_sem.at[1], mate)

    def far_first(slots):
        return sorted(slots, key=lambda s: -place_of(s)[1])

    def hand_own(slot):
        if slot:
            ask(slot).wait_recv()
        for child in far_first(children(ASK, slot)):
            ask(child).start()
        if not wide_ask(slot):
            askx(slot).start()

    def hand_pair(slot):
        (askw if wide_ask(slot) else askx)(slot).wait_recv()
        for child in far_first(children(ASK, slot)):
            if wide_ask(child):
                askw(child).start()

    def choose():
        loads[1].wait()
        loads[2].wait()
        n = parents_v.shape[1]
        entry = table_v[...]
        local = jnp.where(entry // 64 == z, entry % 64, -1).astype(F32).astype(BF16)
        picked = jnp.where(parents_v[...] == iota((n, n), 0), 1.0, 0.0).astype(BF16)
        named = jnp.dot(local, picked, preferred_element_type=F32)
        block = iota((64, n), 0).astype(F32)
        hit = jnp.zeros((64, n), F32)
        for j in range(4):
            hit = jnp.where(named[j : j + 1] == block, 1.0, hit)
        group = jnp.where(iota((n, 128), 0) // BEAMS == iota((n, 128), 1), 1.0, 0.0).astype(BF16)
        count = jnp.dot(hit.astype(BF16), group, preferred_element_type=F32)
        number = iota((32, 128), 0)
        row = iota((8, 128), 0)
        chosen = jnp.zeros((8, 128), jnp.int32)
        for owner in range(2):
            got = count[owner * 32 : owner * 32 + 32] > 0.5
            low = jnp.min(jnp.where(got, number, 32), axis=0, keepdims=True)
            low = jnp.where(low > 31, 0, low) + owner * 32
            high = jnp.max(jnp.where(got, number, 0), axis=0, keepdims=True) + owner * 32
            chosen = jnp.where(row == 2 * owner, low, chosen)
            chosen = jnp.where(row == 2 * owner + 1, high, chosen)
        sel_v[...] = chosen
        to_smem = pltpu.make_async_copy(sel_v, sel_s, local_sem.at[4])
        to_smem.start()
        spread = jnp.where(iota((128, n), 1) // BEAMS == iota((128, n), 0), 1.0, 0.0).astype(BF16)
        wide = jnp.dot(chosen.astype(F32).astype(BF16), spread, preferred_element_type=F32)
        uses = jnp.zeros((8, n), F32)
        for j in range(4):
            uses = jnp.where(named[j : j + 1] == wide, 1.0, uses)
        twin = jnp.concatenate([wide[0:1] - 1.0, wide[0:1], wide[2:3] - 1.0, wide[2:3], wide[4:8]], axis=0)
        wide_row = iota((8, n), 0)
        uses = jnp.where((wide == twin) | (wide_row > 3), 0.0, uses)
        tiled = jnp.concatenate([uses] * NZ, axis=0)
        own = iota((8 * NZ, n), 1) // BEAMS == 2 * (iota((8 * NZ, n), 0) // 8) + core
        tile = jnp.where(iota((n, 256), 0) % BEAMS == iota((n, 256), 1) % BEAMS, 1.0, 0.0).astype(BF16)
        rows = jnp.where(own, tiled, 0.0).astype(BF16)
        keep_v[...] = jnp.where(jnp.dot(rows, tile, preferred_element_type=F32) > 0.5, 0.0, BIG)
        to_smem.wait()

    def vectors(slot):
        return jnp.concatenate([ask_own[slot], ask_pair[slot]], axis=1)

    def suffix(slot):
        sign, d = place_of(slot)
        where = (z - sign * d + NZ) % NZ
        request = 2 * where + core
        blocks = [pool_v[sel_s[k, request]] for k in range(4)]
        keys = jnp.concatenate([b[:, :HD] for b in blocks], axis=0)
        values = jnp.concatenate([b[:, HD:] for b in blocks], axis=0)
        rows = keep_v[pl.ds(pl.multiple_of(where * 8, 8), 8), :]

        def mask(scores):
            return jnp.concatenate(
                [scores[k * HALF : (k + 1) * HALF] + rows[k : k + 1] for k in range(4)], axis=0
            )

        return attend(keys, values, vectors(slot), mask)

    def keep_sums(slot, result):
        part[slot, 0:HD] = result[0]
        part[slot, HD : HD + 1] = result[1]
        part[slot, HD + 1 : HD + 2] = result[2]

    def kept_sums(slot, lanes):
        return (part[slot, 0:HD, lanes], part[slot, HD : HD + 1, lanes], part[slot, HD + 1 : HD + 2, lanes])

    def work(slot):
        result = suffix(slot)
        keep_sums(slot, result)

    def send_on(slot):
        own, other = kept_sums(slot, OWN), kept_sums(slot, OTHER)
        if slot == 0:
            own = combine(own, (run[0:HD, OWN], run[HD : HD + 1, OWN], run[HD + 1 : HD + 2, OWN]))
            other = combine(other, (run[0:HD, OTHER], run[HD : HD + 1, OTHER], run[HD + 1 : HD + 2, OTHER]))
        grown = slot == 0
        for child in children(BACK, slot):
            if wide_back(child):
                back(child).wait_recv()
                own = combine(own, unpack(sum_in.at[child, 0]))
                other = combine(other, unpack(sum_in.at[child, 1]))
                grown = True
        if wide_back(slot):
            pack(sum_out.at[slot, 0], own)
            pack(sum_out.at[slot, 1], other)
            back(slot).start()
        else:
            pack(part_out.at[slot], other)
            partx(slot).start()
            if grown:
                part[slot, 0:HD, OWN] = own[0]
                part[slot, HD : HD + 1, OWN] = own[1]
                part[slot, HD + 1 : HD + 2, OWN] = own[2]

    def merge(slot):
        partx(slot).wait_recv()
        result = combine(kept_sums(slot, OWN), unpack(part_in.at[slot]))
        for child in LAST if slot == 0 else children(BACK, slot):
            if not wide_back(child):
                back(child).wait_recv()
                result = combine(result, unpack(sum_in.at[child, 0]))
        if slot:
            pack(sum_out.at[slot, 0], result)
            back(slot).start()
        return result

    def prompt(i, side):
        lanes = slice(side * HD, (side + 1) * HD)
        start = pl.multiple_of(i * CHUNK, CHUNK)
        rows = prompt_v[pl.ds(start, CHUNK), :]
        inside = iota((HALF, HD), 0)

        def mask(scores):
            parts = []
            for k in range(CHUNK // HALF):
                room = length_ref[0] - 2 * start - (2 * k + half) * HALF
                parts.append(jnp.where(inside < room, scores[k * HALF : (k + 1) * HALF], BIG))
            return jnp.concatenate(parts, axis=0)

        result = attend(rows[:, :HD], rows[:, HD:], (ask_pair if side else ask_own)[0], mask)
        result = combine((run[0:HD, lanes], run[HD : HD + 1, lanes], run[HD + 1 : HD + 2, lanes]), result)
        run[0:HD, lanes] = result[0]
        run[HD : HD + 1, lanes] = result[1]
        run[HD + 1 : HD + 2, lanes] = result[2]

    run[...] = jnp.zeros_like(run)
    run[HD : HD + 1] = jnp.full((1, 256), BIG, F32)
    chunks = prompt_v.shape[0] // CHUNK
    early = z < EARLY

    @pl.when(early)
    def _():
        choose()
        for i, copy in enumerate(prompt_loads):
            copy.wait()
            for k in range(i * 1024 // CHUNK, (i + 1) * 1024 // CHUNK):
                prompt(k, 0)

    pl.semaphore_wait(barrier, len(peers))
    loaded = set()
    for kind, s in ORDER:
        if kind == "h":
            hand_own(s)
            if s == 0:
                to_mate.start()
        elif kind == "w":
            hand_pair(s)
        elif kind == "c":
            pl.when(~early)(choose)
        elif kind == "a":
            if "pool" not in loaded:
                loads[3].wait()
                to_mate.wait()
                loaded.add("pool")
            work(s)
        elif kind == "o":
            send_on(s)
        elif kind == "p":
            piece = s % chunks * CHUNK // 1024
            if piece not in loaded:
                pl.when(~early)(prompt_loads[piece].wait)
                loaded.add(piece)
            if s < chunks:
                pl.when(~early)(functools.partial(prompt, s, 0))
            else:
                prompt(s - chunks, 1)
        elif kind == "m" and s:
            merge(s)
    result = merge(0)
    final = (result[0] / result[2]).T
    for h in range(HEADS):
        out_ref[:, h * HD : (h + 1) * HD] = final[h * BEAMS : (h + 1) * BEAMS, :]
    for s in range(SLOTS):
        if not wide_ask(s):
            askx(s).wait_send()
        if not wide_back(s):
            partx(s).wait_send()
        if s:
            ask(s).wait_send()
            back(s).wait_send()
            if wide_ask(s):
                askw(s).wait_send()


def on_device(queries, prompt_cache, pool, block_table, parents, lengths):
    rows = block_table.shape[0]
    any_space = pl.BlockSpec(memory_space=pl.ANY)
    dma = pltpu.SemaphoreType.DMA
    return pl.pallas_call(
        kernel,
        out_shape=pltpu.VMEM((BEAMS, HEADS * HD), F32),
        in_specs=[pl.BlockSpec(memory_space=pltpu.SMEM)] + [any_space] * 5,
        out_specs=pl.BlockSpec(memory_space=pltpu.VMEM),
        scratch_shapes=[
            pltpu.VMEM((BEAMS, HEADS * HD), BF16),
            pltpu.VMEM((4096, 2 * HD), BF16),
            pltpu.VMEM((64, HALF, 2 * HD), BF16),
            pltpu.VMEM((4, rows), jnp.int32),
            pltpu.VMEM((1, rows), jnp.int32),
            pltpu.VMEM((8, 128), jnp.int32),
            pltpu.SMEM((8, 128), jnp.int32),
            pltpu.VMEM((8 * NZ, 256), F32),
            pltpu.VMEM((SLOTS, HD, HD), BF16),
            pltpu.VMEM((SLOTS, HD, HD), BF16),
            pltpu.VMEM((SLOTS, HD + 8, 2 * HD), F32),
            pltpu.VMEM((SLOTS, MSG, HD), BF16),
            pltpu.VMEM((SLOTS, MSG, HD), BF16),
            pltpu.VMEM((SLOTS, 2, MSG, HD), BF16),
            pltpu.VMEM((SLOTS, 2, MSG, HD), BF16),
            pltpu.VMEM((HD + 8, 2 * HD), F32),
            dma((5,)),
            dma((4,)),
            dma((2,)),
        ]
        + [dma((SLOTS,))] * 10,
        compiler_params=pltpu.CompilerParams(
            collective_id=0, has_side_effects=True, vmem_limit_bytes=54 * 1024 * 1024
        ),
        name="carried_queries",
    )(
        lengths,
        queries,
        prompt_cache[0, 0],
        pool[:, 0],
        block_table.T,
        parents.reshape(1, rows),
    )


def solution(mesh):
    return jax.shard_map(
        on_device,
        mesh=mesh,
        in_specs=(
            P("batch", "mp"),
            P("batch", "mp", None, None),
            P("batch", "mp", None, None),
            P(),
            P(),
            P("batch"),
        ),
        out_specs=P("batch", "mp"),
        check_vma=False,
    )
```

```python
import functools
import math

import jax
import jax.numpy as jnp
from jax import lax
from jax.experimental import pallas as pl
from jax.experimental.pallas import tpu as pltpu
from jax.sharding import PartitionSpec as P

MESH = pl.DeviceIdType.MESH
F32 = jnp.float32
BF16 = jnp.bfloat16

HD = 128
BEAMS = 16
HEADS = 8
NZ = 16
UP = 8
DOWN = 7
SLOTS = 16
HALF = 64
CHUNK = 512
MSG = 144
EARLY = NZ // 2
BIG = -1.0e30
EXPO = HD**-0.5 * math.log2(math.e)
OWN, OTHER = slice(0, HD), slice(HD, 2 * HD)

ASK = {1: 2, 2: 0, 3: 2, 4: 0, 5: 4, 6: 5, 7: 4, 8: 7}
BACK = {1: 0, 2: 3, 3: 0, 4: 5, 5: 6, 6: 0, 7: 6, 8: 6}
ASK_WIDE = (3, 6, 8)
BACK_WIDE = (2, 4, 5, 7)
ORDER = (
    ("h", 0), ("p", 1), ("c", 0), ("p", 0), ("p", 2), ("p", 3), ("p", 4), ("w", 0), ("p", 5), ("p", 11),
    ("p", 6), ("p", 7), ("p", 8), ("p", 9), ("p", 10), ("h", 2), ("h", 10), ("a", 0), ("h", 4), ("h", 12),
    ("p", 12), ("p", 13), ("p", 14), ("p", 15), ("w", 2), ("h", 1), ("o", 0), ("a", 2), ("h", 9), ("h", 11),
    ("w", 10), ("h", 3), ("w", 4), ("o", 2), ("a", 4), ("w", 12), ("o", 4), ("h", 5), ("h", 13), ("a", 12),
    ("o", 12), ("h", 7), ("a", 10), ("h", 15), ("o", 10), ("w", 3), ("w", 11), ("a", 3), ("w", 9), ("w", 1),
    ("a", 11), ("a", 1), ("w", 5), ("o", 3), ("o", 1), ("w", 13), ("a", 5), ("w", 7), ("a", 7), ("o", 7),
    ("h", 14), ("w", 15), ("h", 6), ("a", 15), ("o", 5), ("h", 8), ("o", 15), ("a", 13), ("w", 6), ("o", 13),
    ("m", 3), ("o", 11), ("w", 14), ("m", 1), ("w", 8), ("a", 8), ("o", 8), ("a", 6), ("a", 14), ("a", 9),
    ("o", 6), ("o", 9), ("m", 11), ("o", 14), ("m", 8), ("m", 9), ("m", 14), ("m", 6),
)


LAST = (1, 9, 3, 11, 6, 14)


def slot_of(sign, distance):
    return distance if sign > 0 else UP + distance


def place_of(slot):
    return (1, slot) if slot <= UP else (-1, slot - UP)


def children(table, slot):
    if slot == 0:
        return [s for s in range(1, SLOTS) if table[place_of(s)[1]] == 0]
    sign, distance = place_of(slot)
    return [s for s in range(1, SLOTS) if place_of(s)[0] == sign and table[place_of(s)[1]] == distance]


def wide_ask(slot):
    return slot > 0 and place_of(slot)[1] in ASK_WIDE


def wide_back(slot):
    return slot > 0 and place_of(slot)[1] in BACK_WIDE


def iota(shape, dim):
    return lax.broadcasted_iota(jnp.int32, shape, dim)


def split3(value):
    first = value.astype(BF16).astype(F32)
    rest = value - first
    second = rest.astype(BF16).astype(F32)
    return (first, second, rest - second)


def pack(ref, result):
    acc, top, total = result
    row = iota((16, HD), 0)
    extra = jnp.zeros((16, HD), F32)
    for i, value in enumerate(split3(top) + split3(total)):
        extra = jnp.where(row == i, value, extra)
    ref[0:HD] = acc.astype(BF16)
    ref[HD:MSG] = extra.astype(BF16)


def unpack(ref):
    extra = ref[HD:MSG].astype(F32)
    top = extra[0:1] + extra[1:2] + extra[2:3]
    total = extra[3:4] + extra[4:5] + extra[5:6]
    return (ref[0:HD].astype(F32), top, total)


def combine(a, b):
    top = jnp.maximum(a[1], b[1])
    scale_a = jnp.exp2((a[1] - top) * EXPO)
    scale_b = jnp.exp2((b[1] - top) * EXPO)
    return (a[0] * scale_a + b[0] * scale_b, top, a[2] * scale_a + b[2] * scale_b)


def attend(keys, values, vectors, mask):
    scores = mask(jnp.dot(keys, vectors, preferred_element_type=F32))
    top = jnp.max(scores, axis=0, keepdims=True)
    weights = jnp.exp2((scores - top) * EXPO)
    total = jnp.sum(weights, axis=0, keepdims=True)
    acc = lax.dot_general(
        values, weights.astype(BF16), (((0,), (0,)), ((), ())), preferred_element_type=F32
    )
    return (acc, top, total)


def kernel(
    length_ref, q_hbm, prompt_hbm, pool_hbm, table_hbm, parents_hbm, out_ref,
    q_v, prompt_v, pool_v, table_v, parents_v, sel_v, sel_s, keep_v,
    ask_own, ask_pair, part, part_out, part_in, sum_out, sum_in, run,
    local_sem, prompt_sem, mate_sem, ask_ss, ask_rs, askw_ss, askw_rs, askx_ss, askx_rs, partx_ss, partx_rs, sum_ss, sum_rs,
):
    batch = lax.axis_index("batch")
    mp = lax.axis_index("mp")
    z = batch // 2
    core = batch % 2
    half = mp % 2
    pair = (batch, mp + 1 - 2 * half)
    mate = (batch + 1 - 2 * core, mp)

    def along(offset):
        return ((batch + 2 * (offset % NZ)) % (2 * NZ), mp)

    own_pool = pool_v.at[pl.ds(core * 32, 32)]
    loads = [
        pltpu.make_async_copy(q_hbm, q_v, local_sem.at[0]),
        pltpu.make_async_copy(table_hbm, table_v, local_sem.at[1]),
        pltpu.make_async_copy(parents_hbm, parents_v, local_sem.at[2]),
        pltpu.make_async_copy(pool_hbm, own_pool, local_sem.at[3]),
    ]
    for copy in loads:
        copy.start()
    n_prompt = prompt_v.shape[0] // 1024
    prompt_loads = []
    for i in range(n_prompt):
        rows = pl.ds(i * 1024, 1024)
        prompt_loads.append(
            pltpu.make_async_copy(prompt_hbm.at[rows], prompt_v.at[rows], prompt_sem.at[i])
        )
        prompt_loads[-1].start()

    offsets = set()
    for s in range(1, SLOTS):
        sign, d = place_of(s)
        for table in (ASK,):
            offsets.add(sign * (d - table[d]))
            offsets.add(-sign * (d - table[d]))
    peers = [pair, mate] + [along(o) for o in sorted(offsets)]
    barrier = pltpu.get_barrier_semaphore()
    for peer in peers:
        pl.semaphore_signal(barrier, inc=1, device_id=peer, device_id_type=MESH)

    loads[0].wait()
    stacked = jnp.concatenate([q_v[:, h * HD : (h + 1) * HD] for h in range(HEADS)], axis=0)
    ask_own[0] = stacked.astype(F32).T.astype(BF16)

    def remote(src, dst, send, recv, device):
        return pltpu.make_async_remote_copy(
            src_ref=src, dst_ref=dst, send_sem=send, recv_sem=recv, device_id=device, device_id_type=MESH
        )

    def came(table, slot):
        sign, d = place_of(slot)
        source = table[d]
        return (slot_of(sign, source) if source else 0, sign * (source - d))

    def ask(slot):
        source, offset = came(ASK, slot)
        return remote(ask_own.at[source], ask_own.at[slot], ask_ss.at[slot], ask_rs.at[slot], along(-offset))

    def askw(slot):
        source, offset = came(ASK, slot)
        return remote(ask_pair.at[source], ask_pair.at[slot], askw_ss.at[slot], askw_rs.at[slot], along(-offset))

    def askx(slot):
        return remote(ask_own.at[slot], ask_pair.at[slot], askx_ss.at[slot], askx_rs.at[slot], pair)

    def partx(slot):
        return remote(part_out.at[slot], part_in.at[slot], partx_ss.at[slot], partx_rs.at[slot], pair)

    def back(slot):
        _, offset = came(BACK, slot)
        sides = pl.ds(0, 2 if wide_back(slot) else 1)
        return remote(
            sum_out.at[slot, sides], sum_in.at[slot, sides], sum_ss.at[slot], sum_rs.at[slot], along(offset)
        )

    to_mate = remote(pool_hbm, own_pool, mate_sem.at[0], mate_sem.at[1], mate)

    def far_first(slots):
        return sorted(slots, key=lambda s: -place_of(s)[1])

    def hand_own(slot):
        if slot:
            ask(slot).wait_recv()
        for child in far_first(children(ASK, slot)):
            ask(child).start()
        if not wide_ask(slot):
            askx(slot).start()

    def hand_pair(slot):
        (askw if wide_ask(slot) else askx)(slot).wait_recv()
        for child in far_first(children(ASK, slot)):
            if wide_ask(child):
                askw(child).start()

    def choose():
        loads[1].wait()
        loads[2].wait()
        n = parents_v.shape[1]
        entry = table_v[...]
        local = jnp.where(entry // 64 == z, entry % 64, -1).astype(F32).astype(BF16)
        picked = jnp.where(parents_v[...] == iota((n, n), 0), 1.0, 0.0).astype(BF16)
        named = jnp.dot(local, picked, preferred_element_type=F32)
        block = iota((64, n), 0).astype(F32)
        hit = jnp.zeros((64, n), F32)
        for j in range(4):
            hit = jnp.where(named[j : j + 1] == block, 1.0, hit)
        group = jnp.where(iota((n, 128), 0) // BEAMS == iota((n, 128), 1), 1.0, 0.0).astype(BF16)
        count = jnp.dot(hit.astype(BF16), group, preferred_element_type=F32)
        number = iota((32, 128), 0)
        row = iota((8, 128), 0)
        chosen = jnp.zeros((8, 128), jnp.int32)
        for owner in range(2):
            got = count[owner * 32 : owner * 32 + 32] > 0.5
            low = jnp.min(jnp.where(got, number, 32), axis=0, keepdims=True)
            low = jnp.where(low > 31, 0, low) + owner * 32
            high = jnp.max(jnp.where(got, number, 0), axis=0, keepdims=True) + owner * 32
            chosen = jnp.where(row == 2 * owner, low, chosen)
            chosen = jnp.where(row == 2 * owner + 1, high, chosen)
        sel_v[...] = chosen
        to_smem = pltpu.make_async_copy(sel_v, sel_s, local_sem.at[4])
        to_smem.start()
        spread = jnp.where(iota((128, n), 1) // BEAMS == iota((128, n), 0), 1.0, 0.0).astype(BF16)
        wide = jnp.dot(chosen.astype(F32).astype(BF16), spread, preferred_element_type=F32)
        uses = jnp.zeros((8, n), F32)
        for j in range(4):
            uses = jnp.where(named[j : j + 1] == wide, 1.0, uses)
        twin = jnp.concatenate([wide[0:1] - 1.0, wide[0:1], wide[2:3] - 1.0, wide[2:3], wide[4:8]], axis=0)
        wide_row = iota((8, n), 0)
        uses = jnp.where((wide == twin) | (wide_row > 3), 0.0, uses)
        tiled = jnp.concatenate([uses] * NZ, axis=0)
        own = iota((8 * NZ, n), 1) // BEAMS == 2 * (iota((8 * NZ, n), 0) // 8) + core
        tile = jnp.where(iota((n, 256), 0) % BEAMS == iota((n, 256), 1) % BEAMS, 1.0, 0.0).astype(BF16)
        rows = jnp.where(own, tiled, 0.0).astype(BF16)
        keep_v[...] = jnp.where(jnp.dot(rows, tile, preferred_element_type=F32) > 0.5, 0.0, BIG)
        to_smem.wait()

    def vectors(slot):
        return jnp.concatenate([ask_own[slot], ask_pair[slot]], axis=1)

    def suffix(slot):
        sign, d = place_of(slot)
        where = (z - sign * d + NZ) % NZ
        request = 2 * where + core
        blocks = [pool_v[sel_s[k, request]] for k in range(4)]
        keys = jnp.concatenate([b[:, :HD] for b in blocks], axis=0)
        values = jnp.concatenate([b[:, HD:] for b in blocks], axis=0)
        rows = keep_v[pl.ds(pl.multiple_of(where * 8, 8), 8), :]

        def mask(scores):
            return jnp.concatenate(
                [scores[k * HALF : (k + 1) * HALF] + rows[k : k + 1] for k in range(4)], axis=0
            )

        return attend(keys, values, vectors(slot), mask)

    def keep_sums(slot, result):
        part[slot, 0:HD] = result[0]
        part[slot, HD : HD + 1] = result[1]
        part[slot, HD + 1 : HD + 2] = result[2]

    def kept_sums(slot, lanes):
        return (part[slot, 0:HD, lanes], part[slot, HD : HD + 1, lanes], part[slot, HD + 1 : HD + 2, lanes])

    def work(slot):
        result = suffix(slot)
        keep_sums(slot, result)

    def send_on(slot):
        own, other = kept_sums(slot, OWN), kept_sums(slot, OTHER)
        if slot == 0:
            own = combine(own, (run[0:HD, OWN], run[HD : HD + 1, OWN], run[HD + 1 : HD + 2, OWN]))
            other = combine(other, (run[0:HD, OTHER], run[HD : HD + 1, OTHER], run[HD + 1 : HD + 2, OTHER]))
        grown = slot == 0
        for child in children(BACK, slot):
            if wide_back(child):
                back(child).wait_recv()
                own = combine(own, unpack(sum_in.at[child, 0]))
                other = combine(other, unpack(sum_in.at[child, 1]))
                grown = True
        if wide_back(slot):
            pack(sum_out.at[slot, 0], own)
            pack(sum_out.at[slot, 1], other)
            back(slot).start()
        else:
            pack(part_out.at[slot], other)
            partx(slot).start()
            if grown:
                part[slot, 0:HD, OWN] = own[0]
                part[slot, HD : HD + 1, OWN] = own[1]
                part[slot, HD + 1 : HD + 2, OWN] = own[2]

    def merge(slot):
        partx(slot).wait_recv()
        result = combine(kept_sums(slot, OWN), unpack(part_in.at[slot]))
        for child in LAST if slot == 0 else children(BACK, slot):
            if not wide_back(child):
                back(child).wait_recv()
                result = combine(result, unpack(sum_in.at[child, 0]))
        if slot:
            pack(sum_out.at[slot, 0], result)
            back(slot).start()
        return result

    def prompt(i, side):
        lanes = slice(side * HD, (side + 1) * HD)
        start = pl.multiple_of(i * CHUNK, CHUNK)
        rows = prompt_v[pl.ds(start, CHUNK), :]
        inside = iota((HALF, HD), 0)

        def mask(scores):
            parts = []
            for k in range(CHUNK // HALF):
                room = length_ref[0] - 2 * start - (2 * k + half) * HALF
                parts.append(jnp.where(inside < room, scores[k * HALF : (k + 1) * HALF], BIG))
            return jnp.concatenate(parts, axis=0)

        result = attend(rows[:, :HD], rows[:, HD:], (ask_pair if side else ask_own)[0], mask)
        result = combine((run[0:HD, lanes], run[HD : HD + 1, lanes], run[HD + 1 : HD + 2, lanes]), result)
        run[0:HD, lanes] = result[0]
        run[HD : HD + 1, lanes] = result[1]
        run[HD + 1 : HD + 2, lanes] = result[2]

    run[...] = jnp.zeros_like(run)
    run[HD : HD + 1] = jnp.full((1, 256), BIG, F32)
    chunks = prompt_v.shape[0] // CHUNK
    early = z < EARLY

    @pl.when(early)
    def _():
        choose()
        for i, copy in enumerate(prompt_loads):
            copy.wait()
            for k in range(i * 1024 // CHUNK, (i + 1) * 1024 // CHUNK):
                prompt(k, 0)

    pl.semaphore_wait(barrier, len(peers))
    loaded = set()
    for kind, s in ORDER:
        if kind == "h":
            hand_own(s)
            if s == 0:
                to_mate.start()
        elif kind == "w":
            hand_pair(s)
        elif kind == "c":
            pl.when(~early)(choose)
        elif kind == "a":
            if "pool" not in loaded:
                loads[3].wait()
                to_mate.wait()
                loaded.add("pool")
            work(s)
        elif kind == "o":
            send_on(s)
        elif kind == "p":
            piece = s % chunks * CHUNK // 1024
            if piece not in loaded:
                pl.when(~early)(prompt_loads[piece].wait)
                loaded.add(piece)
            if s < chunks:
                pl.when(~early)(functools.partial(prompt, s, 0))
            else:
                prompt(s - chunks, 1)
        elif kind == "m" and s:
            merge(s)
    result = merge(0)
    final = (result[0] / result[2]).T
    for h in range(HEADS):
        out_ref[:, h * HD : (h + 1) * HD] = final[h * BEAMS : (h + 1) * BEAMS, :]
    for s in range(SLOTS):
        if not wide_ask(s):
            askx(s).wait_send()
        if not wide_back(s):
            partx(s).wait_send()
        if s:
            ask(s).wait_send()
            back(s).wait_send()
            if wide_ask(s):
                askw(s).wait_send()


def on_device(queries, prompt_cache, pool, block_table, parents, lengths):
    rows = block_table.shape[0]
    any_space = pl.BlockSpec(memory_space=pl.ANY)
    dma = pltpu.SemaphoreType.DMA
    return pl.pallas_call(
        kernel,
        out_shape=pltpu.VMEM((BEAMS, HEADS * HD), F32),
        in_specs=[pl.BlockSpec(memory_space=pltpu.SMEM)] + [any_space] * 5,
        out_specs=pl.BlockSpec(memory_space=pltpu.VMEM),
        scratch_shapes=[
            pltpu.VMEM((BEAMS, HEADS * HD), BF16),
            pltpu.VMEM((4096, 2 * HD), BF16),
            pltpu.VMEM((64, HALF, 2 * HD), BF16),
            pltpu.VMEM((4, rows), jnp.int32),
            pltpu.VMEM((1, rows), jnp.int32),
            pltpu.VMEM((8, 128), jnp.int32),
            pltpu.SMEM((8, 128), jnp.int32),
            pltpu.VMEM((8 * NZ, 256), F32),
            pltpu.VMEM((SLOTS, HD, HD), BF16),
            pltpu.VMEM((SLOTS, HD, HD), BF16),
            pltpu.VMEM((SLOTS, HD + 8, 2 * HD), F32),
            pltpu.VMEM((SLOTS, MSG, HD), BF16),
            pltpu.VMEM((SLOTS, MSG, HD), BF16),
            pltpu.VMEM((SLOTS, 2, MSG, HD), BF16),
            pltpu.VMEM((SLOTS, 2, MSG, HD), BF16),
            pltpu.VMEM((HD + 8, 2 * HD), F32),
            dma((5,)),
            dma((4,)),
            dma((2,)),
        ]
        + [dma((SLOTS,))] * 10,
        compiler_params=pltpu.CompilerParams(
            collective_id=0, has_side_effects=True, vmem_limit_bytes=54 * 1024 * 1024
        ),
        name="carried_queries",
    )(
        lengths,
        queries,
        prompt_cache[0, 0],
        pool[:, 0],
        block_table.T,
        parents.reshape(1, rows),
    )


def solution(mesh):
    return jax.shard_map(
        on_device,
        mesh=mesh,
        in_specs=(
            P("batch", "mp"),
            P("batch", "mp", None, None),
            P("batch", "mp", None, None),
            P(),
            P(),
            P("batch"),
        ),
        out_specs=P("batch", "mp"),
        check_vma=False,
    )
```
